256 devices in a mesh: sess: 32 (over y, x, core), blk: 8 (over z).
Axes of the slice: x: 4, y: 4, z: 8, core: 2. Of those that a mesh axis runs over, the one named last changes fastest.
Arguments:
- velocity_old: float32 [3, 8, 8, 8, 32768], P(None, None, None, None, ('sess', 'blk')), may hold values from -6 to 6
- conductance: float32 [8, 8, 8, 32768], P(None, None, None, ('sess', 'blk')), may hold values from 0.3 to 3
- donor_rank: int32 [262144], P(('sess', 'blk')), may hold values from 0 to 31, as said below
- donor_elem: int32 [262144], P(('sess', 'blk')), may hold values from 0 to 127
- target_node: int32 [262144], P(('sess', 'blk')), may hold values from 0 to 65535
- iface_weights: float32 [3, 8, 262144], P(None, None, ('sess', 'blk')), may hold values from -2.5 to 2.5
Outputs:
- velocity_new: float32 [3, 8, 8, 8, 32768], P(None, None, None, None, ('sess', 'blk'))
- iface_values: float32 [3, 262144], P(None, ('sess', 'blk'))
The draws below stay inside these ranges and needn't reach their ends.
Inputs may be any that keep to these rules, and one draw needn't show every extreme that they name: `donor_rank`: ranks below 21 form the background session, the others the inner session; every point's donor rank lies in the session other than its own device's. At most 128 points of one device name one donor rank. For each blk index, one rank of each session is named by exactly 128 points of every device of the other session at that blk index. `donor_elem`: indexes the elements of the donor device that has the point's blk index. `target_node`: indexes the nodes of the point's own device.
All inputs are finite; a program needn't handle non-finite values.
Results may differ from the reference program's by a relative error of at most 0.00013.
Values sent between devices are 32-bit elements; how exact they have to be, the bound alone decides.
No kernel may reach another device: no remote copies, remote signals or barrier semaphores. Data moves between devices by JAX's collectives and lax.ppermute only.
A program may use at most 128 MiB of HBM per device.

```python
import math
import jax
import jax.numpy as jnp
from jax import lax

COMPS = 3
PTS = 8
NPASS = 4
EL_DEV = 128
IPTS = 1024
CAP = 128
ELEMS = 32768
POINTS = 262144
N_SESS = 32
N_BLK = 8


def draw_donor_rank(key, part):
    key = jax.random.fold_in(key, 11)
    background = 2 * N_SESS // 3
    inner_count = N_SESS - background
    devices = N_SESS * N_BLK
    key_outer, key_inner, key_rest = jax.random.split(key, 3)
    hot_outer = jax.random.randint(key_outer, (N_BLK,), 0, inner_count)
    hot_inner = jax.random.randint(key_inner, (N_BLK,), 0, background)
    slot_total = (N_SESS - 1) * CAP
    scale_factor = 1 << 15

    def one_device(device):
        sess_index = device // N_BLK
        block_index = device % N_BLK
        is_outer = sess_index < background
        other_count = jnp.where(is_outer, inner_count, background)
        base_rank = jnp.where(is_outer, background, 0)
        hot_rank = jnp.where(is_outer, hot_outer[block_index], hot_inner[block_index])
        device_key = jax.random.fold_in(key_rest, device)
        score_key, order_key = jax.random.split(device_key)
        virtual = jnp.arange(slot_total, dtype=jnp.int32)
        scores = jax.random.randint(score_key, (slot_total,), 0, scale_factor) * slot_total + virtual
        usable = virtual < (other_count - 1) * CAP
        scores = jnp.where(usable, scores, scale_factor * slot_total + slot_total)
        ordered = jnp.argsort(scores, stable=True)
        chosen = ordered[:IPTS - CAP]
        among = chosen // CAP
        picked = jnp.where(among < hot_rank, among, among + 1)
        ranks = jnp.concatenate([jnp.full((CAP,), hot_rank, jnp.int32), picked.astype(jnp.int32)]) + base_rank
        shuffle = jax.random.permutation(order_key, IPTS)
        return ranks[shuffle]
    return jax.vmap(one_device)(jnp.arange(devices, dtype=jnp.int32)).reshape(-1).astype(jnp.int32)


def place_ends(array, key, smallest, high):
    dims = array.shape
    index_at = [jax.random.randint(jax.random.fold_in(key, axis), (), 0, dims[axis]) for axis in range(len(dims))]
    array = array.at[tuple(index_at)].set(smallest)
    longest = dims.index(max(dims))
    index_at[longest] = (index_at[longest] + 1) % dims[longest]
    return array.at[tuple(index_at)].set(high)


def levels(rng, extent, cuts, smallest, top_value):
    def one(axis_at, shards_of):
        heights = jax.random.uniform(jax.random.fold_in(jax.random.fold_in(rng, 6), axis_at), (shards_of,), jnp.float32, smallest / len(cuts), top_value / len(cuts))
        return jnp.repeat(jnp.exp(heights), extent[axis_at] // shards_of).reshape((-1,) + (1,) * (len(extent) - axis_at - 1))

    gain = one(*cuts[0])
    for cut in cuts[1:]:
        gain = gain * one(*cut)
    return gain


def normal_values(stream_key, dims, deviation, most, shards=(), kind=jnp.bfloat16):
    values = deviation * jax.random.normal(stream_key, dims, jnp.float32)
    if shards:
        values = values * levels(stream_key, dims, shards, -0.22, 0.18)
    return jnp.clip(values, -most, most).astype(kind)


def setup_inputs(seed: int = 0) -> dict:
    arg_keys = jax.random.split(jax.random.key(seed), 7)
    velocity_old = normal_values(arg_keys[0], (COMPS, PTS, PTS, PTS, ELEMS), 1.0, 6.0, ((4, 256),), jnp.float32)
    conductance = jnp.clip(jnp.exp(math.log(3.0) - 2.3025851 * jax.random.uniform(arg_keys[1], (PTS, PTS, PTS, ELEMS), jnp.float32) ** levels(arg_keys[1], (PTS, PTS, PTS, ELEMS), ((3, 256),), -0.2, 0.2)), 0.3, 3.0)
    donor_rank = draw_donor_rank(jax.random.fold_in(arg_keys[6], 71), 0)
    donor_elem = place_ends(jax.random.randint(arg_keys[3], (POINTS,), 0, EL_DEV), jax.random.fold_in(arg_keys[3], 1), 0, EL_DEV - 1).astype(jnp.int32)
    target_node = place_ends(jax.random.randint(arg_keys[4], (POINTS,), 0, 512 * EL_DEV), jax.random.fold_in(arg_keys[4], 1), 0, (512 * EL_DEV) - 1).astype(jnp.int32)
    iface_weights = normal_values(arg_keys[5], (3, PTS, POINTS), 0.3, 2.5, ((2, 256),), jnp.float32)
    return dict(velocity_old=velocity_old, conductance=conductance, donor_rank=donor_rank, donor_elem=donor_elem, target_node=target_node, iface_weights=iface_weights)


H_MASS = 1.0
H_STIFF = 4.0
OMEGA = 0.6
TAU = 8.0


def forward_diff(values, direction):
    length = values.shape[direction]
    upper_part = lax.slice_in_dim(values, 1, length, axis=direction)
    lower_part = lax.slice_in_dim(values, 0, length - 1, axis=direction)
    edge_zero = jnp.zeros_like(lax.slice_in_dim(values, 0, 1, axis=direction))
    return jnp.concatenate([upper_part - lower_part, edge_zero], axis=direction)


def backward_adj(fluxes, direction):
    length = fluxes.shape[direction]
    edge_zero = jnp.zeros_like(lax.slice_in_dim(fluxes, 0, 1, axis=direction))
    shifted = jnp.concatenate([edge_zero, lax.slice_in_dim(fluxes, 0, length - 1, axis=direction)], axis=direction)
    return shifted - fluxes


def local_operator(field_now, conduct):
    result = H_MASS * field_now
    for direction in (1, 2, 3):
        result = result + H_STIFF * backward_adj(conduct[None] * forward_diff(field_now, direction), direction)
    return result


def local_diagonal(conduct):
    result = H_MASS + jnp.zeros_like(conduct)
    for direction in (0, 1, 2):
        length = conduct.shape[direction]
        edge_zero = jnp.zeros_like(lax.slice_in_dim(conduct, 0, 1, axis=direction))
        lower_part = lax.slice_in_dim(conduct, 0, length - 1, axis=direction)
        inner_part = jnp.concatenate([lower_part, edge_zero], axis=direction)
        shifted = jnp.concatenate([edge_zero, lower_part], axis=direction)
        result = result + H_STIFF * (inner_part + shifted)
    return result


def assemble(field_now, column):
    top_face = field_now[..., 7, :, :, :-1]
    bottom = field_now[..., 0, :, :, 1:]
    elem_count = field_now.shape[-1]
    joined = (jnp.arange(1, elem_count, dtype=jnp.int32) % column) != 0
    summed = top_face + bottom
    new_top = jnp.where(joined, summed, top_face)
    new_bottom = jnp.where(joined, summed, bottom)
    field_now = field_now.at[..., 7, :, :, :-1].set(new_top)
    return field_now.at[..., 0, :, :, 1:].set(new_bottom)


def reference(velocity_old, conductance, donor_rank, donor_elem, target_node, iface_weights):
    elem_count = velocity_old.shape[-1]
    devices = N_SESS * N_BLK
    point_dev = jnp.arange(devices * IPTS, dtype=jnp.int32) // IPTS
    block_index = point_dev % N_BLK
    donor_global = ((donor_rank * N_BLK + block_index) * EL_DEV + donor_elem).astype(jnp.int32)
    flat_field = velocity_old.reshape(3, 512, elem_count)

    def interpolate(members):
        indices, weights = members
        picked = jnp.take(flat_field, indices, axis=2).reshape(3, 8, 8, 8, -1)
        first_sum = jnp.sum(picked * weights[2][None, None, None], axis=3)
        second_sum = jnp.sum(first_sum * weights[1][None, None], axis=2)
        return jnp.sum(second_sum * weights[0][None], axis=1)

    weight_blocks = iface_weights.reshape(3, 8, devices, IPTS).transpose(2, 0, 1, 3)
    values = lax.map(interpolate, (donor_global.reshape(devices, IPTS), weight_blocks))
    iface_values = values.transpose(1, 0, 2).reshape(3, devices * IPTS)

    node_elem = (point_dev * EL_DEV + target_node // 512).astype(jnp.int32)
    node_rest = (target_node % 512).astype(jnp.int32)
    rhs_local = (H_MASS * velocity_old).reshape(3, 512, elem_count)
    rhs_local = rhs_local.at[:, node_rest, node_elem].add(TAU * iface_values)
    rhs_local = rhs_local.reshape(velocity_old.shape)
    column = EL_DEV * N_BLK
    right_side = assemble(rhs_local, column)
    diagonal = assemble(local_diagonal(conductance), column)
    field_now = velocity_old
    for pass_index in range(NPASS):
        applied = assemble(local_operator(field_now, conductance), column)
        field_now = field_now + OMEGA * (right_side - applied) / diagonal[None]
    return field_now, iface_values
```

```python
import functools

import jax
import jax.numpy as jnp
from jax import lax
from jax.experimental import pallas as pl
from jax.experimental.pallas import tpu as pltpu
from jax.sharding import PartitionSpec as P

NPASS = 4
H_MASS = 1.0
H_STIFF = 4.0
OMEGA = 0.6
TAU = 8.0
PEERS = 32
BLOCKS = 8
BACKGROUND = 21
F32 = jnp.float32
BF16 = jnp.bfloat16
I32 = jnp.int32
NT = (((1,), (1,)), ((), ()))


def iota(shape, dim):
    return lax.broadcasted_iota(I32, shape, dim)


def lane_gather(values, index):
    return jnp.take_along_axis(values, index, axis=1)


def split2(values):
    high = values.astype(BF16)
    return high, (values - high.astype(F32)).astype(BF16)


def other_session():
    sess = lax.axis_index("sess")
    outer = sess < BACKGROUND
    first = jnp.where(outer, BACKGROUND, 0)
    last = jnp.where(outer, PEERS, BACKGROUND)
    return first, last


def pack_kernel(rank_ref, elem_ref, weight_ref, send_ref, pos_ref, low_ref, high_ref):
    rank_iota = iota((PEERS, 128), 0)
    row = iota((128, 256), 0)
    col = iota((128, 256), 1)
    upper = jnp.where((row < col) | (col >= 128), 1.0, 0.0).astype(BF16)
    hits = [rank_ref[r : r + 1, :] == rank_iota for r in range(8)]
    hot = jnp.concatenate([jnp.where(hit, 1.0, 0.0).astype(BF16) for hit in hits], axis=0)
    counts = jnp.dot(hot, upper, preferred_element_type=F32)
    offset = jnp.zeros((PEERS, 128), F32)
    pos_iota = iota((128, 128), 0)
    lane = iota((PEERS, 128), 1).astype(F32)
    at_slot, low, high = [], [], []
    for r in range(8):
        mine = counts[r * PEERS : (r + 1) * PEERS]
        place = jnp.where(hits[r], mine[:, :128] + offset, 0.0)
        pos = jnp.sum(place, axis=0, keepdims=True).astype(I32)
        offset = offset + mine[:, 128:]
        pos_ref[r : r + 1, :] = pos
        at_slot.append(jnp.where(pos == pos_iota, 1.0, 0.0).astype(BF16))
        low.append(jnp.where(hits[r], lane, 0.0).astype(BF16))
        high.append(jnp.where(hits[r], float(r), 0.0).astype(BF16))
    at_slot = jnp.concatenate(at_slot, axis=1)
    both = jnp.concatenate([jnp.concatenate(low, axis=1), jnp.concatenate(high, axis=1)], axis=0)
    inverse = lax.dot_general(both, at_slot, NT, preferred_element_type=F32)
    low_ref[...] = inverse[:PEERS].astype(I32)
    high_ref[...] = inverse[PEERS:].astype(I32)
    first, last = other_session()
    sub = iota((8, 128), 0)
    elems = elem_ref[...].astype(F32)

    def one_peer(peer, carry):
        index = jnp.broadcast_to(low_ref[pl.ds(peer, 1), :], (8, 128))
        part = jnp.broadcast_to(high_ref[pl.ds(peer, 1), :], (8, 128))
        for group in range(3):
            rows = slice(group * 8, group * 8 + 8)
            picked = lane_gather(weight_ref[rows, 0:128], index)
            for r in range(1, 8):
                other = lane_gather(weight_ref[rows, r * 128 : r * 128 + 128], index)
                picked = jnp.where(part == r, other, picked)
            send_ref[peer, rows, :] = picked
        ids = jnp.where(sub == part, lane_gather(elems, index), 0.0)
        send_ref[peer, 24:32, :] = jnp.broadcast_to(jnp.sum(ids, axis=0, keepdims=True), (8, 128))
        return carry

    lax.fori_loop(first, last, one_peer, 0)


def serve_kernel(recv_ref, v_ref, reply_ref):
    first, last = other_session()

    def one_peer(peer, carry):
        index = recv_ref[peer, 24:32, :].astype(I32)
        wz = [jnp.broadcast_to(recv_ref[peer, z : z + 1, :], (8, 128)) for z in range(8)]
        wy = [jnp.broadcast_to(recv_ref[peer, 8 + y : 9 + y, :], (8, 128)) for y in range(8)]
        wx = recv_ref[peer, 16:24, :]
        for c in range(3):
            total = jnp.zeros((8, 128), F32)
            for z in range(8):
                line = jnp.zeros((8, 128), F32)
                for y in range(8):
                    line = line + lane_gather(v_ref[c, z, y], index) * wy[y]
                total = total + line * wz[z]
            reply_ref[peer, c : c + 1, :] = jnp.sum(total * wx, axis=0, keepdims=True)
        return carry

    lax.fori_loop(first, last, one_peer, 0)


def finish_kernel(reply_ref, rank_ref, pos_ref, target_ref, value_ref, ends_ref):
    first, last = other_session()
    ranks = [jnp.broadcast_to(rank_ref[r : r + 1, :], (8, 128)) for r in range(8)]
    index = [jnp.broadcast_to(pos_ref[r : r + 1, :], (8, 128)) for r in range(8)]

    def one_peer(peer, sums):
        have = reply_ref[peer]
        return tuple(
            jnp.where(ranks[r] == peer, lane_gather(have, index[r]), sums[r]) for r in range(8)
        )

    sums = lax.fori_loop(first, last, one_peer, tuple(jnp.zeros((8, 128), F32) for _ in range(8)))
    values = jnp.concatenate(sums, axis=1)
    value_ref[...] = values[0:3]
    target = jnp.concatenate([target_ref[r : r + 1, :] for r in range(8)], axis=1)
    elem = target >> 9
    zx = ((target >> 6) & 7) * 8 + (target & 7)
    y2 = ((target >> 3) & 7) * 2
    key = jnp.where(elem == 127, y2, jnp.where(elem == 0, y2 + 1, -1))
    left = jnp.where(zx == iota((64, 1024), 0), 1.0, 0.0).astype(BF16)
    hit = key == iota((16, 1024), 0)
    rows = jnp.concatenate([jnp.where(hit, values[c : c + 1], 0.0) for c in range(3)], axis=0)
    rows = jnp.concatenate([rows, jnp.zeros((16, 1024), F32)], axis=0)
    high, low = split2(rows)
    both = jnp.concatenate([high, low], axis=0)
    out = lax.dot_general(left, both, NT, preferred_element_type=F32)
    ends_ref[...] = TAU * (out + pltpu.roll(out, 64, 1))


def ends_kernel(v_ref, c_ref, ends_ref):
    lane = iota((8, 128), 1)
    for z in range(8):
        block = jnp.zeros((8, 128), F32)
        for c in range(3):
            for y in range(8):
                i = c * 8 + y
                rolled = pltpu.roll(v_ref[c, z, y], 2 * i + 1, 1)
                block = jnp.where((lane >> 1) == i, rolled, block)
        ends_ref[z * 8 : z * 8 + 8, :] = block
        block = jnp.zeros((8, 128), F32)
        for y in range(8):
            rolled = pltpu.roll(c_ref[z, y], 2 * y + 1, 1)
            block = jnp.where((lane >> 1) == y, rolled, block)
        block = block + pltpu.roll(block, 16, 1) + pltpu.roll(block, 32, 1)
        ends_ref[64 + z * 8 : 72 + z * 8, :] = block


def main_kernel(v_ref, c_ref, value_ref, target_ref, out_ref, rhs_ref, buf_ref, w_ref, k_ref, kx_ref, dl_ref):
    lane = iota((8, 128), 1)
    sub = iota((8, 128), 0)
    target = jnp.concatenate([target_ref[r : r + 1, :] for r in range(8)], axis=1)
    elem = target >> 9
    node = target & 511
    left = jnp.where(node == iota((512, 1024), 0), 1.0, 0.0).astype(BF16)
    hit = elem == iota((128, 1024), 0)
    for c in range(3):
        high, low = split2(jnp.where(hit, TAU * value_ref[c : c + 1, :], 0.0))
        both = jnp.concatenate([high, low], axis=0)
        out = lax.dot_general(left, both, NT, preferred_element_type=F32)
        added = (out[:, :128] + out[:, 128:]).reshape(8, 8, 8, 128)
        rhs_ref[c] = H_MASS * v_ref[c] + added
    for z in range(8):
        for y in range(8):
            k = H_STIFF * c_ref[z, y]
            k_ref[z, y] = k
            kx_ref[z, y] = jnp.where(sub < 7, k, 0.0)
    for y in range(8):
        diags = []
        for z in range(8):
            kx = kx_ref[z, y]
            d = H_MASS + kx + pltpu.roll(kx, 1, 0)
            if z < 7:
                d = d + k_ref[z, y]
            if z > 0:
                d = d + k_ref[z - 1, y]
            if y < 7:
                d = d + k_ref[z, y]
            if y > 0:
                d = d + k_ref[z, y - 1]
            diags.append(d)
        dl_ref[0, y] = diags[0]
        dl_ref[1, y] = diags[7]
        bottom = diags[0] + jnp.where(lane > 0, pltpu.roll(diags[7], 1, 1), 0.0)
        top = diags[7] + jnp.where(lane < 127, pltpu.roll(diags[0], 127, 1), 0.0)
        diags[0], diags[7] = bottom, top
        for z in range(8):
            w_ref[z, y] = OMEGA / diags[z]

    def local_sum(src, c, z, y, v):
        kx = kx_ref[z, y]
        s = rhs_ref[c, z, y] + kx * pltpu.roll(v, 7, 0) + pltpu.roll(kx * v, 1, 0)
        if z < 7:
            s = s + k_ref[z, y] * src[c, z + 1, y]
        if z > 0:
            s = s + k_ref[z - 1, y] * src[c, z - 1, y]
        if y < 7:
            s = s + k_ref[z, y] * src[c, z, y + 1]
        if y > 0:
            s = s + k_ref[z, y - 1] * src[c, z, y - 1]
        return s

    def one_pass(src, dst):
        for y in range(8):
            for z in range(1, 7):
                for c in range(3):
                    v = src[c, z, y]
                    s = local_sum(src, c, z, y, v)
                    dst[c, z, y] = (1.0 - OMEGA) * v + w_ref[z, y] * s
            for c in range(3):
                v0 = src[c, 0, y]
                v7 = src[c, 7, y]
                r0 = local_sum(src, c, 0, y, v0) - dl_ref[0, y] * v0
                r7 = local_sum(src, c, 7, y, v7) - dl_ref[1, y] * v7
                s0 = r0 + jnp.where(lane > 0, pltpu.roll(r7, 1, 1), 0.0)
                s7 = r7 + jnp.where(lane < 127, pltpu.roll(r0, 127, 1), 0.0)
                dst[c, 0, y] = v0 + w_ref[0, y] * s0
                dst[c, 7, y] = v7 + w_ref[7, y] * s7

    one_pass(v_ref, buf_ref)
    one_pass(buf_ref, out_ref)
    one_pass(out_ref, buf_ref)
    one_pass(buf_ref, out_ref)


def edge_kernel(main_ref, own_ref, below_ref, above_ref, add_ref, add_below_ref, add_above_ref, out_ref):
    blk = lax.axis_index("blk")
    lane = iota((8, 128), 1)
    sub = iota((8, 128), 0)
    even = (lane & 1) == 0
    joined = (even & (blk < BLOCKS - 1)) | (jnp.logical_not(even) & (blk > 0))
    y_of = (lane >> 1) & 7

    def stack(own, below, above, offset):
        lower, upper = [], []
        for z in range(8):
            rows = slice(offset + z * 8, offset + z * 8 + 8)
            mine = own[rows, :]
            lower.append(jnp.where(even, mine, pltpu.roll(below[rows, :], 1, 1)))
            upper.append(jnp.where(even, pltpu.roll(above[rows, :], 127, 1), mine))
        return lower + upper

    v = stack(own_ref, below_ref, above_ref, 0)
    cond = stack(own_ref, below_ref, above_ref, 64)
    add = stack(add_ref, add_below_ref, add_above_ref, 0)
    rhs = [H_MASS * v[i] + add[i] for i in range(16)]
    k = [H_STIFF * cond[i] for i in range(16)]
    kz = [k[i] if i % 8 < 7 else None for i in range(16)]
    ky = [jnp.where(y_of < 7, k[i], 0.0) for i in range(16)]
    kx = [jnp.where(sub < 7, k[i], 0.0) for i in range(16)]
    diag = []
    for i in range(16):
        d = H_MASS + kx[i] + pltpu.roll(kx[i], 1, 0) + ky[i] + pltpu.roll(ky[i], 2, 1)
        if kz[i] is not None:
            d = d + kz[i]
        if i % 8 > 0:
            d = d + kz[i - 1]
        diag.append(d)
    d7, d8 = diag[7], diag[8]
    full = list(diag)
    full[7] = d7 + jnp.where(joined, d8, 0.0)
    full[8] = d8 + jnp.where(joined, d7, 0.0)
    w = [OMEGA / d for d in full]
    for _ in range(NPASS):
        r = []
        for i in range(16):
            s = rhs[i] + kx[i] * pltpu.roll(v[i], 7, 0) + pltpu.roll(kx[i] * v[i], 1, 0)
            s = s + ky[i] * pltpu.roll(v[i], 126, 1) + pltpu.roll(ky[i] * v[i], 2, 1)
            if kz[i] is not None:
                s = s + kz[i] * v[i + 1]
            if i % 8 > 0:
                s = s + kz[i - 1] * v[i - 1]
            r.append(s - diag[i] * v[i])
        r7, r8 = r[7], r[8]
        r[7] = r7 + jnp.where(joined, r8, 0.0)
        r[8] = r8 + jnp.where(joined, r7, 0.0)
        v = [v[i] + w[i] * r[i] for i in range(16)]
    for c in range(3):
        for y in range(8):
            i = c * 8 + y
            back = (128 - (2 * i + 1)) % 128
            for z in range(8):
                new = v[z] if z >= 4 else v[8 + z]
                where = lane == (127 if z >= 4 else 0)
                out_ref[c, z, y] = jnp.where(where, pltpu.roll(new, back, 1), main_ref[c, z, y])


def call(kernel, outs, args, scratch=(), limit=24, **kw):
    single = len(outs) == 1
    spec = pl.BlockSpec(memory_space=pltpu.VMEM)
    return pl.pallas_call(
        kernel,
        out_shape=outs[0] if single else outs,
        in_specs=[spec] * len(args),
        out_specs=spec if single else [spec] * len(outs),
        scratch_shapes=list(scratch),
        compiler_params=pltpu.CompilerParams(vmem_limit_bytes=limit * 1024 * 1024),
        **kw,
    )(*args)


def sds(*shape, dtype=F32):
    return jax.ShapeDtypeStruct(shape, dtype)


def body(velocity_old, conductance, donor_rank, donor_elem, target_node, iface_weights):
    rank = donor_rank.reshape(8, 128)
    elem = donor_elem.reshape(8, 128)
    target = target_node.reshape(8, 128)
    weights = iface_weights.reshape(24, 1024)
    send, pos = call(
        pack_kernel,
        [sds(PEERS, 32, 128), sds(8, 128, dtype=I32)],
        [rank, elem, weights],
        [pltpu.VMEM((PEERS, 128), I32), pltpu.VMEM((PEERS, 128), I32)],
    )
    up = [(i, (i + 1) % BLOCKS) for i in range(BLOCKS)]
    down = [(j, i) for i, j in up]
    recv = lax.all_to_all(send, "sess", 0, 0, tiled=True)
    own = call(ends_kernel, [sds(128, 128)], [velocity_old, conductance])
    below = lax.ppermute(own, "blk", up)
    above = lax.ppermute(own, "blk", down)
    reply = call(serve_kernel, [sds(PEERS, 8, 128)], [recv, velocity_old])
    reply = lax.all_to_all(reply, "sess", 0, 0, tiled=True)
    iface_values, add = call(
        finish_kernel, [sds(3, 1024), sds(64, 128)], [reply, rank, pos, target]
    )
    add_below = lax.ppermute(add, "blk", up)
    add_above = lax.ppermute(add, "blk", down)
    plane = (8, 8, 8, 128)
    main = call(
        main_kernel,
        [sds(3, *plane)],
        [velocity_old, conductance, iface_values, target],
        [
            pltpu.VMEM((3,) + plane, F32),
            pltpu.VMEM((3,) + plane, F32),
            pltpu.VMEM(plane, F32),
            pltpu.VMEM(plane, F32),
            pltpu.VMEM(plane, F32),
            pltpu.VMEM((2, 8, 8, 128), F32),
        ],
        limit=32,
    )
    field = call(
        edge_kernel,
        [sds(3, *plane)],
        [main, own, below, above, add, add_below, add_above],
    )
    return field, iface_values


def solution(mesh):
    in_specs = (
        P(None, None, None, None, ("sess", "blk")),
        P(None, None, None, ("sess", "blk")),
        P(("sess", "blk")),
        P(("sess", "blk")),
        P(("sess", "blk")),
        P(None, None, ("sess", "blk")),
    )
    out_specs = (P(None, None, None, None, ("sess", "blk")), P(None, ("sess", "blk")))
    return jax.shard_map(body, mesh=mesh, in_specs=in_specs, out_specs=out_specs, check_vma=False)
```

```python
import jax
import jax.numpy as jnp
from jax import lax
from jax.experimental import pallas as pl
from jax.experimental.pallas import tpu as pltpu
from jax.sharding import PartitionSpec as P

NPASS = 4
H_MASS = 1.0
H_STIFF = 4.0
OMEGA = 0.6
TAU = 8.0
PEERS = 32
BLOCKS = 8
BACKGROUND = 21
F32 = jnp.float32
BF16 = jnp.bfloat16
I32 = jnp.int32
NT = (((1,), (1,)), ((), ()))


def iota(shape, dim):
    return lax.broadcasted_iota(I32, shape, dim)


def lane_gather(values, index):
    return jnp.take_along_axis(values, index, axis=1)


def split2(values):
    high = values.astype(BF16)
    return high, (values - high.astype(F32)).astype(BF16)


def pack_kernel(
    rank_hbm, elem_hbm, weight_hbm, target_hbm, send_ref, meta_ref, rank_ref, elem_ref, weight_ref, target_ref, low_ref, high_ref, sems
):
    copies = [
        pltpu.make_async_copy(rank_hbm, rank_ref, sems.at[0]),
        pltpu.make_async_copy(elem_hbm, elem_ref, sems.at[1]),
        pltpu.make_async_copy(weight_hbm, weight_ref, sems.at[2]),
        pltpu.make_async_copy(target_hbm, target_ref, sems.at[3]),
    ]
    for copy in copies:
        copy.start()
    copies[0].wait()
    rank_iota = iota((PEERS, 128), 0)
    row = iota((128, 256), 0)
    col = iota((128, 256), 1)
    upper = jnp.where((row < col) | (col >= 128), 1.0, 0.0).astype(BF16)
    hits = [rank_ref[r : r + 1, :] == rank_iota for r in range(8)]
    hot = jnp.concatenate([jnp.where(hit, 1.0, 0.0).astype(BF16) for hit in hits], axis=0)
    counts = jnp.dot(hot, upper, preferred_element_type=F32)
    offset = jnp.zeros((PEERS, 128), F32)
    pos_iota = iota((128, 128), 0)
    lane = iota((PEERS, 128), 1).astype(F32)
    at_slot, low, high = [], [], []
    for r in range(8):
        mine = counts[r * PEERS : (r + 1) * PEERS]
        place = jnp.where(hits[r], mine[:, :128] + offset, 0.0)
        pos = jnp.sum(place, axis=0, keepdims=True).astype(I32)
        offset = offset + mine[:, 128:]
        meta_ref[r : r + 1, :] = pos
        at_slot.append(jnp.where(pos == pos_iota, 1.0, 0.0).astype(BF16))
        low.append(jnp.where(hits[r], lane, 0.0).astype(BF16))
        high.append(jnp.where(hits[r], float(r), 0.0).astype(BF16))
    at_slot = jnp.concatenate(at_slot, axis=1)
    both = jnp.concatenate([jnp.concatenate(low, axis=1), jnp.concatenate(high, axis=1)], axis=0)
    inverse = lax.dot_general(both, at_slot, NT, preferred_element_type=F32)
    low_ref[...] = inverse[:PEERS].astype(I32)
    high_ref[...] = inverse[PEERS:].astype(I32)
    for copy in copies[1:]:
        copy.wait()
    meta_ref[8:16, :] = rank_ref[...]
    meta_ref[16:24, :] = target_ref[...]
    outer = lax.axis_index("sess") < BACKGROUND
    first = jnp.where(outer, BACKGROUND, 0)
    turns = jnp.where(outer, 1, 2)
    sub = iota((8, 128), 0)
    elems = elem_ref[...].astype(F32)

    def some_peers(turn, carry):
        for step in range(PEERS - BACKGROUND):
            peer = first + turn * (PEERS - BACKGROUND) + step
            index = jnp.broadcast_to(low_ref[pl.ds(peer, 1), :], (8, 128))
            part = jnp.broadcast_to(high_ref[pl.ds(peer, 1), :], (8, 128))
            for group in range(3):
                rows = slice(group * 8, group * 8 + 8)
                picked = lane_gather(weight_ref[rows, 0:128], index)
                for r in range(1, 8):
                    other = lane_gather(weight_ref[rows, r * 128 : r * 128 + 128], index)
                    picked = jnp.where(part == r, other, picked)
                send_ref[pl.ds(peer * 25 + group * 8, 8), :] = picked
            ids = jnp.where(sub == part, lane_gather(elems, index), 0.0)
            send_ref[pl.ds(peer * 25 + 24, 1), :] = jnp.sum(ids, axis=0, keepdims=True)
        return carry

    lax.fori_loop(0, turns, some_peers, 0)


def serve_kernel(recv_ref, split_ref, first_ref, reply_ref):
    outer = lax.axis_index("sess") < BACKGROUND
    first = jnp.where(outer, BACKGROUND - 1, 0)
    turns = jnp.where(outer, 3, 6)
    elem_iota = iota((128, 128), 0)

    def four_peers(turn, carry):
        peers = [first + turn * 4 + i for i in range(4)]
        hot, picks = [], []
        for peer in peers:
            index = recv_ref[pl.ds(peer * 25 + 24, 1), :].astype(I32)
            picks.append(jnp.broadcast_to(index, (8, 128)))
            hot.append(jnp.where(index == elem_iota, 1.0, 0.0).astype(BF16))
        hot = jnp.concatenate(hot, axis=1)
        hot = jnp.concatenate([hot, hot], axis=0)

        def weight(peer, i):
            return jnp.broadcast_to(recv_ref[pl.ds(peer * 25 + i, 1), :], (8, 128))

        for c in range(3):
            if c:
                rows = slice(c * 512 - 512, c * 512)
                picked = jnp.dot(split_ref[rows, :], hot, preferred_element_type=F32).reshape(8, 8, 8, 512)
            for i, peer in enumerate(peers):
                total = None
                for z in range(8):
                    line = None
                    for y in range(8):
                        if c:
                            term = picked[z, y, :, i * 128 : i * 128 + 128]
                        else:
                            term = lane_gather(first_ref[z, y], picks[i])
                        term = term * weight(peer, 8 + y)
                        line = term if line is None else line + term
                    line = line * weight(peer, z)
                    total = line if total is None else total + line
                wx = recv_ref[pl.ds(peer * 25 + 16, 8), :]
                reply_ref[pl.ds(peer * 3 + c, 1), :] = jnp.sum(total * wx, axis=0, keepdims=True)
        return carry

    lax.fori_loop(0, turns, four_peers, 0)


def finish_kernel(reply_ref, meta_ref, value_ref, copy_ref, low_ref, high_ref):
    sub = iota((8, 128), 0)
    planes = [[reply_ref[pl.ds(g * 24 + c, 8, stride=3), :] for g in range(4)] for c in range(3)]
    values = [[], [], []]
    for r in range(8):
        index = jnp.broadcast_to(meta_ref[r : r + 1, :], (8, 128))
        rank = jnp.broadcast_to(meta_ref[8 + r : 9 + r, :], (8, 128))
        for c in range(3):
            total = jnp.zeros((8, 128), F32)
            for g in range(4):
                total = jnp.where(rank == sub + 8 * g, lane_gather(planes[c][g], index), total)
            values[c].append(jnp.sum(total, axis=0, keepdims=True))
    values = jnp.concatenate([jnp.concatenate(v, axis=1) for v in values], axis=0)
    value_ref[...] = values
    copy_ref[...] = values
    target = jnp.concatenate([meta_ref[16 + r : 17 + r, :] for r in range(8)], axis=1)
    elem = target >> 9
    zx = ((target >> 6) & 7) * 8 + (target & 7)
    y2 = ((target >> 3) & 7) * 2
    key = jnp.where(elem == 127, y2, jnp.where(elem == 0, y2 + 1, -1))
    left = jnp.where(zx == iota((64, 1024), 0), 1.0, 0.0).astype(BF16)
    hit = key == iota((16, 1024), 0)
    rows = jnp.concatenate([jnp.where(hit, values[c : c + 1], 0.0) for c in range(3)], axis=0)
    rows = jnp.concatenate([rows, jnp.zeros((16, 1024), F32)], axis=0)
    high, low = split2(rows)
    both = jnp.concatenate([high, low], axis=0)
    out = lax.dot_general(left, both, NT, preferred_element_type=F32)
    out = TAU * (out + pltpu.roll(out, 64, 1))
    low_ref[...] = out[:32]
    high_ref[...] = out[32:]


def ends_kernel(v_ref, c_ref, ends_ref, split_ref, first_ref):
    first_ref[...] = v_ref[0]
    lane = iota((8, 128), 1)
    for c in (1, 2):
        high, low = split2(v_ref[c].reshape(512, 128))
        split_ref[c * 512 - 512 : c * 512, 0:128] = high
        split_ref[c * 512 - 512 : c * 512, 128:256] = low
    for z in range(8):
        block = jnp.zeros((8, 128), F32)
        for c in range(3):
            for y in range(8):
                i = c * 8 + y
                rolled = pltpu.roll(v_ref[c, z, y], 2 * i + 1, 1)
                block = jnp.where((lane >> 1) == i, rolled, block)
        ends_ref[z * 8 : z * 8 + 8, :] = block
        block = jnp.zeros((8, 128), F32)
        for y in range(8):
            rolled = pltpu.roll(c_ref[z, y], 2 * y + 1, 1)
            block = jnp.where((lane >> 1) == y, rolled, block)
        block = block + pltpu.roll(block, 16, 1) + pltpu.roll(block, 32, 1)
        ends_ref[64 + z * 8 : 72 + z * 8, :] = block


def neighbour_sum(c_ref, kx, src, c, z, y, v):
    s = kx * pltpu.roll(v, 7, 0) + pltpu.roll(kx * v, 1, 0)
    if z < 7:
        s = s + c_ref[z, y] * src[c, z + 1, y]
    if z > 0:
        s = s + c_ref[z - 1, y] * src[c, z - 1, y]
    if y < 7:
        s = s + c_ref[z, y] * src[c, z, y + 1]
    if y > 0:
        s = s + c_ref[z, y - 1] * src[c, z, y - 1]
    return s


def local_diag(c_ref, z, y):
    kx = jnp.where(iota((8, 128), 0) < 7, c_ref[z, y], 0.0)
    d = H_MASS / H_STIFF + kx + pltpu.roll(kx, 1, 0)
    if z < 7:
        d = d + c_ref[z, y]
    if z > 0:
        d = d + c_ref[z - 1, y]
    if y < 7:
        d = d + c_ref[z, y]
    if y > 0:
        d = d + c_ref[z, y - 1]
    return d


def couple(lower, upper, lane):
    to_upper = upper + jnp.where(lane > 0, pltpu.roll(lower, 1, 1), 0.0)
    to_lower = lower + jnp.where(lane < 127, pltpu.roll(upper, 127, 1), 0.0)
    return to_lower, to_upper


def one_pass(c_ref, w_ref, dl_ref, rhs, src, dst, extra=None):
    lane = iota((8, 128), 1)
    sub = iota((8, 128), 0)

    def store(c, z, y, value):
        dst[c, z, y] = value if extra is None else value + extra[c, z, y]

    for y in range(8):
        for z in range(1, 7):
            kx = jnp.where(sub < 7, c_ref[z, y], 0.0)
            for c in range(3):
                v = src[c, z, y]
                s = rhs(c, z, y) + neighbour_sum(c_ref, kx, src, c, z, y, v)
                store(c, z, y, (1.0 - OMEGA) * v + w_ref[z, y] * s)
        k0 = jnp.where(sub < 7, c_ref[0, y], 0.0)
        k7 = jnp.where(sub < 7, c_ref[7, y], 0.0)
        for c in range(3):
            v0 = src[c, 0, y]
            v7 = src[c, 7, y]
            r0 = rhs(c, 0, y) + neighbour_sum(c_ref, k0, src, c, 0, y, v0) - dl_ref[0, y] * v0
            r7 = rhs(c, 7, y) + neighbour_sum(c_ref, k7, src, c, 7, y, v7) - dl_ref[1, y] * v7
            s7, s0 = couple(r7, r0, lane)
            store(c, 0, y, v0 + w_ref[0, y] * s0)
            store(c, 7, y, v7 + w_ref[7, y] * s7)


def edge_masks():
    blk = lax.axis_index("blk")
    even = (iota((8, 128), 1) & 1) == 0
    joined = (even & (blk < BLOCKS - 1)) | (jnp.logical_not(even) & (blk > 0))
    return even, joined


def edge_stack(own, below, above, offset, even):
    lower, upper = [], []
    for z in range(8):
        rows = slice(offset + z * 8, offset + z * 8 + 8)
        mine = own[rows, :]
        lower.append(jnp.where(even, mine, pltpu.roll(below[rows, :], 1, 1)))
        upper.append(jnp.where(even, pltpu.roll(above[rows, :], 127, 1), mine))
    return lower + upper


def edge_pass(number, v, rhs, k, ky, kx, w, d7, d8, joined):
    r = {}
    for i in range(1 + number, 15 - number):
        s = rhs[i]
        s = s + kx[i] * pltpu.roll(v[i], 7, 0) + pltpu.roll(kx[i] * v[i], 1, 0)
        s = s + ky[i] * pltpu.roll(v[i], 126, 1) + pltpu.roll(ky[i] * v[i], 2, 1)
        if i % 8 < 7:
            s = s + k[i] * v[i + 1]
        if i % 8 > 0:
            s = s + k[i - 1] * v[i - 1]
        if i == 7:
            s = s - d7 * v[i]
        if i == 8:
            s = s - d8 * v[i]
        r[i] = s
    r[7], r[8] = r[7] + jnp.where(joined, r[8], 0.0), r[8] + jnp.where(joined, r[7], 0.0)
    return {i: (v[i] if i in (7, 8) else (1.0 - OMEGA) * v[i]) + w[i] * r[i] for i in r}


def base_kernel(v_ref, c_ref, meta_ref, out_ref, w_ref, node_ref, buf_ref, dl_ref):
    lane = iota((8, 128), 1)
    target = jnp.concatenate([meta_ref[16 + r : 17 + r, :] for r in range(8)], axis=1)
    node_ref[...] = jnp.where((target & 511) == iota((512, 1024), 0), 1.0, 0.0).astype(BF16)
    for y in range(8):
        diags = [local_diag(c_ref, z, y) for z in range(8)]
        dl_ref[0, y] = diags[0]
        dl_ref[1, y] = diags[7]
        diags[7], diags[0] = couple(diags[7], diags[0], lane)
        for z in range(8):
            w_ref[z, y] = OMEGA / diags[z]

    def rhs(c, z, y):
        return (H_MASS / H_STIFF) * v_ref[c, z, y]

    coefs = (c_ref, w_ref, dl_ref, rhs)
    one_pass(*coefs, v_ref, buf_ref)
    one_pass(*coefs, buf_ref, out_ref)
    one_pass(*coefs, out_ref, buf_ref)
    one_pass(*coefs, buf_ref, out_ref)


def main_kernel(value_ref, meta_ref, node_ref, base_ref, w_ref, c_ref, out_ref, add_ref, one_ref, two_ref, dl_ref):
    lane = iota((8, 128), 1)
    target = jnp.concatenate([meta_ref[16 + r : 17 + r, :] for r in range(8)], axis=1)
    elem_hot = jnp.where((target >> 9) == iota((128, 1024), 0), 1.0, 0.0).astype(BF16)
    for c in range(3):
        value = (TAU / H_STIFF) * value_ref[c : c + 1, :]
        high, low = split2(jnp.broadcast_to(value, (16, 1024)))
        high = elem_hot * jnp.concatenate([high] * 8, axis=0)
        low = elem_hot * jnp.concatenate([low] * 8, axis=0)
        both = jnp.concatenate([high, low], axis=0)
        out = lax.dot_general(node_ref[...], both, NT, preferred_element_type=F32)
        add_ref[c] = (out[:, :128] + out[:, 128:]).reshape(8, 8, 8, 128)
    for y in range(8):
        dl_ref[0, y] = local_diag(c_ref, 0, y)
        dl_ref[1, y] = local_diag(c_ref, 7, y)
        for z in range(1, 7):
            for c in range(3):
                one_ref[c, z, y] = w_ref[z, y] * add_ref[c, z, y]
        for c in range(3):
            s7, s0 = couple(add_ref[c, 7, y], add_ref[c, 0, y], lane)
            one_ref[c, 0, y] = w_ref[0, y] * s0
            one_ref[c, 7, y] = w_ref[7, y] * s7

    def rhs(c, z, y):
        return add_ref[c, z, y]

    coefs = (c_ref, w_ref, dl_ref, rhs)
    one_pass(*coefs, one_ref, two_ref)
    one_pass(*coefs, two_ref, one_ref)
    one_pass(*coefs, one_ref, out_ref, base_ref)


def edge_kernel(
    main_ref, own_ref, below_ref, above_ref, low_ref, high_ref, add_below_ref, add_above_ref, out_ref
):
    lane = iota((8, 128), 1)
    sub = iota((8, 128), 0)
    even, joined = edge_masks()
    y_of = (lane >> 1) & 7
    v = edge_stack(own_ref, below_ref, above_ref, 0, even)
    k = [H_STIFF * c for c in edge_stack(own_ref, below_ref, above_ref, 64, even)]
    rhs = [H_MASS * v[i] for i in range(16)]
    for z in range(8):
        part, rows = (low_ref, high_ref)[z // 4], slice(z % 4 * 8, z % 4 * 8 + 8)
        mine = part[rows, :]
        lower, upper = jnp.where(even, mine, 0.0), jnp.where(even, 0.0, mine)
        if z >= 4:
            lower = jnp.where(even, mine, pltpu.roll(add_below_ref[rows, :], 1, 1))
        else:
            upper = jnp.where(even, pltpu.roll(add_above_ref[rows, :], 127, 1), mine)
        rhs[z] = rhs[z] + lower
        rhs[8 + z] = rhs[8 + z] + upper
    ky = [jnp.where(y_of < 7, k[i], 0.0) for i in range(16)]
    kx = [jnp.where(sub < 7, k[i], 0.0) for i in range(16)]
    diag = []
    for i in range(16):
        d = H_MASS + kx[i] + pltpu.roll(kx[i], 1, 0) + ky[i] + pltpu.roll(ky[i], 2, 1)
        if i % 8 < 7:
            d = d + k[i]
        if i % 8 > 0:
            d = d + k[i - 1]
        diag.append(d)
    d7, d8 = diag[7], diag[8]
    diag[7], diag[8] = d7 + jnp.where(joined, d8, 0.0), d8 + jnp.where(joined, d7, 0.0)
    w = [OMEGA / d for d in diag]
    now = v
    for number in range(NPASS):
        now = edge_pass(number, now, rhs, k, ky, kx, w, d7, d8, joined)
    for c in range(3):
        for y in range(8):
            back = (127 - 2 * (c * 8 + y)) % 128
            for z in range(8):
                new = now[z] if z >= 4 else now[8 + z]
                where = lane == (127 if z >= 4 else 0)
                out_ref[c, z, y] = jnp.where(where, pltpu.roll(new, back, 1), main_ref[c, z, y])


def exchange(rows, count):
    chunks = rows.reshape(PEERS, count, 1, 128)
    return lax.all_to_all(chunks, "sess", 0, 0, tiled=True).reshape(PEERS * count, 128)


def call(kernel, outs, args, scratch=(), limit=24, space=pltpu.VMEM, cost=None):
    single = len(outs) == 1
    spec = pl.BlockSpec(memory_space=pltpu.VMEM)
    return pl.pallas_call(
        kernel,
        out_shape=outs[0] if single else outs,
        in_specs=[pl.BlockSpec(memory_space=space)] * len(args),
        out_specs=spec if single else [spec] * len(outs),
        scratch_shapes=list(scratch),
        compiler_params=pltpu.CompilerParams(vmem_limit_bytes=limit * 1024 * 1024),
        cost_estimate=cost,
    )(*args)


def sds(*shape, dtype=F32):
    return jax.ShapeDtypeStruct(shape, dtype)


def body(velocity_old, conductance, donor_rank, donor_elem, target_node, iface_weights):
    rank = donor_rank.reshape(8, 128)
    elem = donor_elem.reshape(8, 128)
    target = target_node.reshape(8, 128)
    weights = iface_weights.reshape(24, 1024)
    send, meta = call(
        pack_kernel,
        [sds(PEERS * 25, 128), sds(24, 128, dtype=I32)],
        [rank, elem, weights, target],
        [
            pltpu.VMEM((8, 128), I32),
            pltpu.VMEM((8, 128), I32),
            pltpu.VMEM((24, 1024), F32),
            pltpu.VMEM((8, 128), I32),
            pltpu.VMEM((PEERS, 128), I32),
            pltpu.VMEM((PEERS, 128), I32),
            pltpu.SemaphoreType.DMA((4,)),
        ],
        space=pl.ANY,
        limit=56,
    )
    up = [(i, (i + 1) % BLOCKS) for i in range(BLOCKS)]
    down = [(j, i) for i, j in up]
    recv = exchange(send, 25)
    plane = (8, 8, 8, 128)
    own, split, first = call(
        ends_kernel,
        [sds(128, 128), sds(1024, 256, dtype=BF16), sds(*plane)],
        [velocity_old, conductance],
    )
    below = lax.ppermute(own, "blk", up)
    above = lax.ppermute(own, "blk", down)
    base, w, nodes = call(
        base_kernel,
        [sds(3, *plane), sds(*plane), sds(512, 1024, dtype=BF16)],
        [velocity_old, conductance, meta],
        [pltpu.VMEM((3,) + plane, F32), pltpu.VMEM((2, 8, 8, 128), F32)],
        cost=pl.CostEstimate(flops=20_000_000, bytes_accessed=6_000_000, transcendentals=0),
    )
    recv, below, above, base, w, nodes = lax.optimization_barrier(
        (recv, below, above, base, w, nodes)
    )
    reply = call(serve_kernel, [sds(PEERS * 3, 128)], [recv, split, first])
    reply = exchange(reply, 3)
    iface_values, values, add_low, add_high = call(
        finish_kernel, [sds(3, 1024), sds(3, 1024), sds(32, 128), sds(32, 128)], [reply, meta]
    )
    add_below = lax.ppermute(add_high, "blk", up)
    add_above = lax.ppermute(add_low, "blk", down)
    main = call(
        main_kernel,
        [sds(3, *plane)],
        [values, meta, nodes, base, w, conductance],
        [pltpu.VMEM((3,) + plane, F32)] * 3 + [pltpu.VMEM((2, 8, 8, 128), F32)],
        cost=pl.CostEstimate(flops=20_000_000, bytes_accessed=6_000_000, transcendentals=0),
    )
    field = call(
        edge_kernel, [sds(3, *plane)], [main, own, below, above, add_low, add_high, add_below, add_above]
    )
    return field, iface_values


def solution(mesh):
    in_specs = (
        P(None, None, None, None, ("sess", "blk")),
        P(None, None, None, ("sess", "blk")),
        P(("sess", "blk")),
        P(("sess", "blk")),
        P(("sess", "blk")),
        P(None, None, ("sess", "blk")),
    )
    out_specs = (P(None, None, None, None, ("sess", "blk")), P(None, ("sess", "blk")))
    return jax.shard_map(body, mesh=mesh, in_specs=in_specs, out_specs=out_specs, check_vma=False)
```

```python
import jax
import jax.numpy as jnp
from jax import lax
from jax.experimental import pallas as pl
from jax.experimental.pallas import tpu as pltpu
from jax.sharding import PartitionSpec as P

NPASS = 4
H_MASS = 1.0
H_STIFF = 4.0
OMEGA = 0.6
TAU = 8.0
PEERS = 32
BLOCKS = 8
BACKGROUND = 21
F32 = jnp.float32
BF16 = jnp.bfloat16
I32 = jnp.int32
NT = (((1,), (1,)), ((), ()))


def iota(shape, dim):
    return lax.broadcasted_iota(I32, shape, dim)


def lane_gather(values, index):
    return jnp.take_along_axis(values, index, axis=1)


def split2(values):
    high = values.astype(BF16)
    return high, (values - high.astype(F32)).astype(BF16)


def pack_kernel(
    rank_hbm, elem_hbm, weight_hbm, target_hbm, send_ref, meta_ref, rank_ref, elem_ref, weight_ref, target_ref, low_ref, high_ref, sems
):
    copies = [
        pltpu.make_async_copy(rank_hbm, rank_ref, sems.at[0]),
        pltpu.make_async_copy(elem_hbm, elem_ref, sems.at[1]),
        pltpu.make_async_copy(weight_hbm, weight_ref, sems.at[2]),
        pltpu.make_async_copy(target_hbm, target_ref, sems.at[3]),
    ]
    for copy in copies:
        copy.start()
    copies[0].wait()
    rank_iota = iota((PEERS, 128), 0)
    row = iota((128, 256), 0)
    col = iota((128, 256), 1)
    upper = jnp.where((row < col) | (col >= 128), 1.0, 0.0).astype(BF16)
    hits = [rank_ref[r : r + 1, :] == rank_iota for r in range(8)]
    hot = jnp.concatenate([jnp.where(hit, 1.0, 0.0).astype(BF16) for hit in hits], axis=0)
    counts = jnp.dot(hot, upper, preferred_element_type=F32)
    offset = jnp.zeros((PEERS, 128), F32)
    pos_iota = iota((128, 128), 0)
    lane = iota((PEERS, 128), 1).astype(F32)
    at_slot, low, high = [], [], []
    for r in range(8):
        mine = counts[r * PEERS : (r + 1) * PEERS]
        place = jnp.where(hits[r], mine[:, :128] + offset, 0.0)
        pos = jnp.sum(place, axis=0, keepdims=True).astype(I32)
        offset = offset + mine[:, 128:]
        meta_ref[r : r + 1, :] = pos
        at_slot.append(jnp.where(pos == pos_iota, 1.0, 0.0).astype(BF16))
        low.append(jnp.where(hits[r], lane, 0.0).astype(BF16))
        high.append(jnp.where(hits[r], float(r), 0.0).astype(BF16))
    at_slot = jnp.concatenate(at_slot, axis=1)
    both = jnp.concatenate([jnp.concatenate(low, axis=1), jnp.concatenate(high, axis=1)], axis=0)
    inverse = lax.dot_general(both, at_slot, NT, preferred_element_type=F32)
    low_ref[...] = inverse[:PEERS].astype(I32)
    high_ref[...] = inverse[PEERS:].astype(I32)
    for copy in copies[1:]:
        copy.wait()
    meta_ref[8:16, :] = rank_ref[...]
    meta_ref[16:24, :] = target_ref[...]
    outer = lax.axis_index("sess") < BACKGROUND
    first = jnp.where(outer, BACKGROUND, 0)
    turns = jnp.where(outer, 1, 2)
    sub = iota((8, 128), 0)
    elems = elem_ref[...].astype(F32)

    def some_peers(turn, carry):
        for step in range(PEERS - BACKGROUND):
            peer = first + turn * (PEERS - BACKGROUND) + step
            index = jnp.broadcast_to(low_ref[pl.ds(peer, 1), :], (8, 128))
            part = jnp.broadcast_to(high_ref[pl.ds(peer, 1), :], (8, 128))
            for group in range(3):
                rows = slice(group * 8, group * 8 + 8)
                picked = lane_gather(weight_ref[rows, 0:128], index)
                for r in range(1, 8):
                    other = lane_gather(weight_ref[rows, r * 128 : r * 128 + 128], index)
                    picked = jnp.where(part == r, other, picked)
                send_ref[pl.ds(peer * 25 + group * 8, 8), :] = picked
            ids = jnp.where(sub == part, lane_gather(elems, index), 0.0)
            send_ref[pl.ds(peer * 25 + 24, 1), :] = jnp.sum(ids, axis=0, keepdims=True)
        return carry

    lax.fori_loop(0, turns, some_peers, 0)


def serve_kernel(recv_ref, split_ref, first_ref, reply_ref):
    outer = lax.axis_index("sess") < BACKGROUND
    first = jnp.where(outer, PEERS - 14, 0)
    turns = jnp.where(outer, 2, 3)
    elem_iota = iota((128, 128), 0)

    def seven_peers(turn, carry):
        peers = [first + turn * 7 + i for i in range(7)]
        hot, picks = [], []
        for peer in peers:
            index = recv_ref[pl.ds(peer * 25 + 24, 1), :].astype(I32)
            picks.append(jnp.broadcast_to(index, (8, 128)))
            hot.append(jnp.where(index == elem_iota, 1.0, 0.0).astype(BF16))
        hot = jnp.concatenate(hot, axis=1)
        hot = jnp.concatenate([hot, hot], axis=0)

        def weight(peer, i):
            return jnp.broadcast_to(recv_ref[pl.ds(peer * 25 + i, 1), :], (8, 128))

        for c in range(3):
            if c:
                rows = slice(c * 512 - 512, c * 512)
                picked = jnp.dot(split_ref[rows, :], hot, preferred_element_type=F32).reshape(8, 8, 8, 896)
            for i, peer in enumerate(peers):
                total = None
                for z in range(8):
                    line = None
                    for y in range(8):
                        if c:
                            term = picked[z, y, :, i * 128 : i * 128 + 128]
                        else:
                            term = lane_gather(first_ref[z, y], picks[i])
                        term = term * weight(peer, 8 + y)
                        line = term if line is None else line + term
                    line = line * weight(peer, z)
                    total = line if total is None else total + line
                wx = recv_ref[pl.ds(peer * 25 + 16, 8), :]
                reply_ref[pl.ds(peer * 3 + c, 1), :] = jnp.sum(total * wx, axis=0, keepdims=True)
        return carry

    lax.fori_loop(0, turns, seven_peers, 0)


def finish_kernel(reply_ref, meta_ref, value_ref, copy_ref, low_ref, high_ref):
    sub = iota((8, 128), 0)
    planes = [[reply_ref[pl.ds(g * 24 + c, 8, stride=3), :] for g in range(4)] for c in range(3)]
    values = [[], [], []]
    for r in range(8):
        index = jnp.broadcast_to(meta_ref[r : r + 1, :], (8, 128))
        rank = jnp.broadcast_to(meta_ref[8 + r : 9 + r, :], (8, 128))
        for c in range(3):
            total = jnp.zeros((8, 128), F32)
            for g in range(4):
                total = jnp.where(rank == sub + 8 * g, lane_gather(planes[c][g], index), total)
            values[c].append(jnp.sum(total, axis=0, keepdims=True))
    values = jnp.concatenate([jnp.concatenate(v, axis=1) for v in values], axis=0)
    value_ref[...] = values
    copy_ref[...] = values
    target = jnp.concatenate([meta_ref[16 + r : 17 + r, :] for r in range(8)], axis=1)
    elem = target >> 9
    zx = ((target >> 6) & 7) * 8 + (target & 7)
    y2 = ((target >> 3) & 7) * 2
    key = jnp.where(elem == 127, y2, jnp.where(elem == 0, y2 + 1, -1))
    left = jnp.where(zx == iota((64, 1024), 0), 1.0, 0.0).astype(BF16)
    hit = key == iota((16, 1024), 0)
    rows = jnp.concatenate([jnp.where(hit, values[c : c + 1], 0.0) for c in range(3)], axis=0)
    rows = jnp.concatenate([rows, jnp.zeros((16, 1024), F32)], axis=0)
    high, low = split2(rows)
    both = jnp.concatenate([high, low], axis=0)
    out = lax.dot_general(left, both, NT, preferred_element_type=F32)
    out = TAU * (out + pltpu.roll(out, 64, 1))
    low_ref[...] = out[:32]
    high_ref[...] = out[32:]


def ends_kernel(v_ref, c_ref, ends_ref, split_ref, first_ref):
    first_ref[...] = v_ref[0]
    lane = iota((8, 128), 1)
    for c in (1, 2):
        high, low = split2(v_ref[c].reshape(512, 128))
        split_ref[c * 512 - 512 : c * 512, 0:128] = high
        split_ref[c * 512 - 512 : c * 512, 128:256] = low
    for z in range(8):
        block = jnp.zeros((8, 128), F32)
        for c in range(3):
            for y in range(8):
                i = c * 8 + y
                rolled = pltpu.roll(v_ref[c, z, y], 2 * i + 1, 1)
                block = jnp.where((lane >> 1) == i, rolled, block)
        ends_ref[z * 8 : z * 8 + 8, :] = block
        block = jnp.zeros((8, 128), F32)
        for y in range(8):
            rolled = pltpu.roll(c_ref[z, y], 2 * y + 1, 1)
            block = jnp.where((lane >> 1) == y, rolled, block)
        block = block + pltpu.roll(block, 16, 1) + pltpu.roll(block, 32, 1)
        ends_ref[64 + z * 8 : 72 + z * 8, :] = block


def neighbour_sum(c_ref, kx, src, c, z, y, v):
    s = kx * pltpu.roll(v, 7, 0) + pltpu.roll(kx * v, 1, 0)
    if z < 7:
        s = s + c_ref[z, y] * src[c, z + 1, y]
    if z > 0:
        s = s + c_ref[z - 1, y] * src[c, z - 1, y]
    if y < 7:
        s = s + c_ref[z, y] * src[c, z, y + 1]
    if y > 0:
        s = s + c_ref[z, y - 1] * src[c, z, y - 1]
    return s


def local_diag(c_ref, z, y):
    kx = jnp.where(iota((8, 128), 0) < 7, c_ref[z, y], 0.0)
    d = H_MASS / H_STIFF + kx + pltpu.roll(kx, 1, 0)
    if z < 7:
        d = d + c_ref[z, y]
    if z > 0:
        d = d + c_ref[z - 1, y]
    if y < 7:
        d = d + c_ref[z, y]
    if y > 0:
        d = d + c_ref[z, y - 1]
    return d


def couple(lower, upper, lane):
    to_upper = upper + jnp.where(lane > 0, pltpu.roll(lower, 1, 1), 0.0)
    to_lower = lower + jnp.where(lane < 127, pltpu.roll(upper, 127, 1), 0.0)
    return to_lower, to_upper


def one_pass(c_ref, w_ref, dl_ref, rhs, src, dst, extra=None):
    lane = iota((8, 128), 1)
    sub = iota((8, 128), 0)

    def store(c, z, y, value):
        dst[c, z, y] = value if extra is None else value + extra[c, z, y]

    for y in range(8):
        for z in range(1, 7):
            kx = jnp.where(sub < 7, c_ref[z, y], 0.0)
            for c in range(3):
                v = src[c, z, y]
                s = rhs(c, z, y) + neighbour_sum(c_ref, kx, src, c, z, y, v)
                store(c, z, y, (1.0 - OMEGA) * v + w_ref[z, y] * s)
        k0 = jnp.where(sub < 7, c_ref[0, y], 0.0)
        k7 = jnp.where(sub < 7, c_ref[7, y], 0.0)
        for c in range(3):
            v0 = src[c, 0, y]
            v7 = src[c, 7, y]
            r0 = rhs(c, 0, y) + neighbour_sum(c_ref, k0, src, c, 0, y, v0) - dl_ref[0, y] * v0
            r7 = rhs(c, 7, y) + neighbour_sum(c_ref, k7, src, c, 7, y, v7) - dl_ref[1, y] * v7
            s7, s0 = couple(r7, r0, lane)
            store(c, 0, y, v0 + w_ref[0, y] * s0)
            store(c, 7, y, v7 + w_ref[7, y] * s7)


def edge_masks():
    blk = lax.axis_index("blk")
    even = (iota((8, 128), 1) & 1) == 0
    joined = (even & (blk < BLOCKS - 1)) | (jnp.logical_not(even) & (blk > 0))
    return even, joined


def edge_stack(own, below, above, offset, even):
    lower, upper = [], []
    for z in range(8):
        rows = slice(offset + z * 8, offset + z * 8 + 8)
        mine = own[rows, :]
        lower.append(jnp.where(even, mine, pltpu.roll(below[rows, :], 1, 1)))
        upper.append(jnp.where(even, pltpu.roll(above[rows, :], 127, 1), mine))
    return lower + upper


def edge_pass(number, v, rhs, k, ky, kx, w, d7, d8, joined):
    r = {}
    for i in range(1 + number, 15 - number):
        s = rhs[i]
        s = s + kx[i] * pltpu.roll(v[i], 7, 0) + pltpu.roll(kx[i] * v[i], 1, 0)
        s = s + ky[i] * pltpu.roll(v[i], 126, 1) + pltpu.roll(ky[i] * v[i], 2, 1)
        if i % 8 < 7:
            s = s + k[i] * v[i + 1]
        if i % 8 > 0:
            s = s + k[i - 1] * v[i - 1]
        if i == 7:
            s = s - d7 * v[i]
        if i == 8:
            s = s - d8 * v[i]
        r[i] = s
    r[7], r[8] = r[7] + jnp.where(joined, r[8], 0.0), r[8] + jnp.where(joined, r[7], 0.0)
    return {i: (v[i] if i in (7, 8) else (1.0 - OMEGA) * v[i]) + w[i] * r[i] for i in r}


def base_kernel(v_ref, c_ref, meta_ref, out_ref, w_ref, node_ref, buf_ref, dl_ref):
    lane = iota((8, 128), 1)
    target = jnp.concatenate([meta_ref[16 + r : 17 + r, :] for r in range(8)], axis=1)
    node_ref[...] = jnp.where((target & 511) == iota((512, 1024), 0), 1.0, 0.0).astype(BF16)
    for y in range(8):
        diags = [local_diag(c_ref, z, y) for z in range(8)]
        dl_ref[0, y] = diags[0]
        dl_ref[1, y] = diags[7]
        diags[7], diags[0] = couple(diags[7], diags[0], lane)
        for z in range(8):
            w_ref[z, y] = OMEGA / diags[z]

    def rhs(c, z, y):
        return (H_MASS / H_STIFF) * v_ref[c, z, y]

    coefs = (c_ref, w_ref, dl_ref, rhs)
    one_pass(*coefs, v_ref, buf_ref)
    one_pass(*coefs, buf_ref, out_ref)
    one_pass(*coefs, out_ref, buf_ref)
    one_pass(*coefs, buf_ref, out_ref)


def main_kernel(value_ref, meta_ref, node_ref, base_ref, w_ref, c_ref, out_ref, add_ref, one_ref, two_ref, dl_ref):
    lane = iota((8, 128), 1)
    target = jnp.concatenate([meta_ref[16 + r : 17 + r, :] for r in range(8)], axis=1)
    elem_hot = jnp.where((target >> 9) == iota((128, 1024), 0), 1.0, 0.0).astype(BF16)
    for c in range(3):
        value = (TAU / H_STIFF) * value_ref[c : c + 1, :]
        high, low = split2(jnp.broadcast_to(value, (16, 1024)))
        high = elem_hot * jnp.concatenate([high] * 8, axis=0)
        low = elem_hot * jnp.concatenate([low] * 8, axis=0)
        both = jnp.concatenate([high, low], axis=0)
        out = lax.dot_general(node_ref[...], both, NT, preferred_element_type=F32)
        add_ref[c] = (out[:, :128] + out[:, 128:]).reshape(8, 8, 8, 128)
    for y in range(8):
        dl_ref[0, y] = local_diag(c_ref, 0, y)
        dl_ref[1, y] = local_diag(c_ref, 7, y)
        for z in range(1, 7):
            for c in range(3):
                one_ref[c, z, y] = w_ref[z, y] * add_ref[c, z, y]
        for c in range(3):
            s7, s0 = couple(add_ref[c, 7, y], add_ref[c, 0, y], lane)
            one_ref[c, 0, y] = w_ref[0, y] * s0
            one_ref[c, 7, y] = w_ref[7, y] * s7

    def rhs(c, z, y):
        return add_ref[c, z, y]

    coefs = (c_ref, w_ref, dl_ref, rhs)
    one_pass(*coefs, one_ref, two_ref)
    one_pass(*coefs, two_ref, one_ref)
    one_pass(*coefs, one_ref, out_ref, base_ref)


def edge_kernel(
    main_ref, own_ref, below_ref, above_ref, low_ref, high_ref, add_below_ref, add_above_ref, out_hbm, out_ref, sems
):
    lane = iota((8, 128), 1)
    sub = iota((8, 128), 0)
    even, joined = edge_masks()
    y_of = (lane >> 1) & 7
    v = edge_stack(own_ref, below_ref, above_ref, 0, even)
    k = [H_STIFF * c for c in edge_stack(own_ref, below_ref, above_ref, 64, even)]
    rhs = [H_MASS * v[i] for i in range(16)]
    for z in range(8):
        part, rows = (low_ref, high_ref)[z // 4], slice(z % 4 * 8, z % 4 * 8 + 8)
        mine = part[rows, :]
        lower, upper = jnp.where(even, mine, 0.0), jnp.where(even, 0.0, mine)
        if z >= 4:
            lower = jnp.where(even, mine, pltpu.roll(add_below_ref[rows, :], 1, 1))
        else:
            upper = jnp.where(even, pltpu.roll(add_above_ref[rows, :], 127, 1), mine)
        rhs[z] = rhs[z] + lower
        rhs[8 + z] = rhs[8 + z] + upper
    ky = [jnp.where(y_of < 7, k[i], 0.0) for i in range(16)]
    kx = [jnp.where(sub < 7, k[i], 0.0) for i in range(16)]
    diag = []
    for i in range(16):
        d = H_MASS + kx[i] + pltpu.roll(kx[i], 1, 0) + ky[i] + pltpu.roll(ky[i], 2, 1)
        if i % 8 < 7:
            d = d + k[i]
        if i % 8 > 0:
            d = d + k[i - 1]
        diag.append(d)
    d7, d8 = diag[7], diag[8]
    diag[7], diag[8] = d7 + jnp.where(joined, d8, 0.0), d8 + jnp.where(joined, d7, 0.0)
    w = [OMEGA / d for d in diag]
    now = v
    for number in range(NPASS):
        now = edge_pass(number, now, rhs, k, ky, kx, w, d7, d8, joined)
    copies = []
    for c in range(3):
        for half in range(2):
            planes = slice(half * 4, half * 4 + 4)
            for y in range(8):
                back = (127 - 2 * (c * 8 + y)) % 128
                where = lane == (0, 127)[half]
                for z in range(half * 4, half * 4 + 4):
                    new = pltpu.roll(now[z] if half else now[8 + z], back, 1)
                    out_ref[c, z, y] = jnp.where(where, new, main_ref[c, z, y])
            copies.append(
                pltpu.make_async_copy(
                    out_ref.at[c, planes], out_hbm.at[c, planes], sems.at[2 * c + half]
                )
            )
            copies[-1].start()
    for copy in copies:
        copy.wait()


def exchange(rows, count):
    chunks = rows.reshape(PEERS, count, 1, 128)
    return lax.all_to_all(chunks, "sess", 0, 0, tiled=True).reshape(PEERS * count, 128)


def call(kernel, outs, args, scratch=(), limit=24, space=pltpu.VMEM, out_space=pltpu.VMEM):
    single = len(outs) == 1
    spec = pl.BlockSpec(memory_space=out_space)
    return pl.pallas_call(
        kernel,
        out_shape=outs[0] if single else outs,
        in_specs=[pl.BlockSpec(memory_space=space)] * len(args),
        out_specs=spec if single else [spec] * len(outs),
        scratch_shapes=list(scratch),
        compiler_params=pltpu.CompilerParams(vmem_limit_bytes=limit * 1024 * 1024),
    )(*args)


def sds(*shape, dtype=F32):
    return jax.ShapeDtypeStruct(shape, dtype)


def body(velocity_old, conductance, donor_rank, donor_elem, target_node, iface_weights):
    rank = donor_rank.reshape(8, 128)
    elem = donor_elem.reshape(8, 128)
    target = target_node.reshape(8, 128)
    weights = iface_weights.reshape(24, 1024)
    send, meta = call(
        pack_kernel,
        [sds(PEERS * 25, 128), sds(24, 128, dtype=I32)],
        [rank, elem, weights, target],
        [
            pltpu.VMEM((8, 128), I32),
            pltpu.VMEM((8, 128), I32),
            pltpu.VMEM((24, 1024), F32),
            pltpu.VMEM((8, 128), I32),
            pltpu.VMEM((PEERS, 128), I32),
            pltpu.VMEM((PEERS, 128), I32),
            pltpu.SemaphoreType.DMA((4,)),
        ],
        space=pl.ANY,
        limit=56,
    )
    up = [(i, (i + 1) % BLOCKS) for i in range(BLOCKS)]
    down = [(j, i) for i, j in up]
    recv = exchange(send, 25)
    plane = (8, 8, 8, 128)
    own, split, first = call(
        ends_kernel,
        [sds(128, 128), sds(1024, 256, dtype=BF16), sds(*plane)],
        [velocity_old, conductance],
    )
    below = lax.ppermute(own, "blk", up)
    above = lax.ppermute(own, "blk", down)
    recv, below, above = lax.optimization_barrier((recv, below, above))
    reply = call(serve_kernel, [sds(PEERS * 3, 128)], [recv, split, first])
    reply, v_later, c_later = lax.optimization_barrier((reply, velocity_old, conductance))
    reply = exchange(reply, 3)
    base, w, nodes = call(
        base_kernel,
        [sds(3, *plane), sds(*plane), sds(512, 1024, dtype=BF16)],
        [v_later, c_later, meta],
        [pltpu.VMEM((3,) + plane, F32), pltpu.VMEM((2, 8, 8, 128), F32)],
    )
    reply, base, w, nodes = lax.optimization_barrier((reply, base, w, nodes))
    iface_values, values, add_low, add_high = call(
        finish_kernel, [sds(3, 1024), sds(3, 1024), sds(32, 128), sds(32, 128)], [reply, meta]
    )
    add_below = lax.ppermute(add_high, "blk", up)
    add_above = lax.ppermute(add_low, "blk", down)
    main = call(
        main_kernel,
        [sds(3, *plane)],
        [values, meta, nodes, base, w, c_later],
        [pltpu.VMEM((3,) + plane, F32)] * 3 + [pltpu.VMEM((2, 8, 8, 128), F32)],
    )
    field = call(
        edge_kernel,
        [sds(3, *plane)],
        [main, own, below, above, add_low, add_high, add_below, add_above],
        [pltpu.VMEM((3,) + plane, F32), pltpu.SemaphoreType.DMA((6,))],
        out_space=pl.ANY,
    )
    return field, iface_values


def solution(mesh):
    in_specs = (
        P(None, None, None, None, ("sess", "blk")),
        P(None, None, None, ("sess", "blk")),
        P(("sess", "blk")),
        P(("sess", "blk")),
        P(("sess", "blk")),
        P(None, None, ("sess", "blk")),
    )
    out_specs = (P(None, None, None, None, ("sess", "blk")), P(None, ("sess", "blk")))
    return jax.shard_map(body, mesh=mesh, in_specs=in_specs, out_specs=out_specs, check_vma=False)
```

```python
import jax
import jax.numpy as jnp
from jax import lax
from jax.experimental import pallas as pl
from jax.experimental.pallas import tpu as pltpu
from jax.sharding import PartitionSpec as P

NPASS = 4
H_MASS = 1.0
H_STIFF = 4.0
OMEGA = 0.6
TAU = 8.0
PEERS = 32
BLOCKS = 8
BACKGROUND = 21
F32 = jnp.float32
BF16 = jnp.bfloat16
I32 = jnp.int32
NT = (((1,), (1,)), ((), ()))


def iota(shape, dim):
    return lax.broadcasted_iota(I32, shape, dim)


def lane_gather(values, index):
    return jnp.take_along_axis(values, index, axis=1)


def split2(values):
    high = values.astype(BF16)
    return high, (values - high.astype(F32)).astype(BF16)


def pack_kernel(
    rank_hbm, elem_hbm, weight_hbm, target_hbm, send_ref, meta_ref, rank_ref, elem_ref, weight_ref, target_ref, low_ref, high_ref, sems
):
    copies = [
        pltpu.make_async_copy(rank_hbm, rank_ref, sems.at[0]),
        pltpu.make_async_copy(elem_hbm, elem_ref, sems.at[1]),
        pltpu.make_async_copy(weight_hbm, weight_ref, sems.at[2]),
        pltpu.make_async_copy(target_hbm, target_ref, sems.at[3]),
    ]
    for copy in copies:
        copy.start()
    copies[0].wait()
    rank_iota = iota((PEERS, 128), 0)
    row = iota((128, 256), 0)
    col = iota((128, 256), 1)
    upper = jnp.where((row < col) | (col >= 128), 1.0, 0.0).astype(BF16)
    hits = [rank_ref[r : r + 1, :] == rank_iota for r in range(8)]
    hot = jnp.concatenate([jnp.where(hit, 1.0, 0.0).astype(BF16) for hit in hits], axis=0)
    counts = jnp.dot(hot, upper, preferred_element_type=F32)
    offset = jnp.zeros((PEERS, 128), F32)
    pos_iota = iota((128, 128), 0)
    lane = iota((PEERS, 128), 1).astype(F32)
    at_slot, low, high = [], [], []
    for r in range(8):
        mine = counts[r * PEERS : (r + 1) * PEERS]
        place = jnp.where(hits[r], mine[:, :128] + offset, 0.0)
        pos = jnp.sum(place, axis=0, keepdims=True).astype(I32)
        offset = offset + mine[:, 128:]
        meta_ref[r : r + 1, :] = pos
        at_slot.append(jnp.where(pos == pos_iota, 1.0, 0.0).astype(BF16))
        low.append(jnp.where(hits[r], lane, 0.0).astype(BF16))
        high.append(jnp.where(hits[r], float(r), 0.0).astype(BF16))
    at_slot = jnp.concatenate(at_slot, axis=1)
    both = jnp.concatenate([jnp.concatenate(low, axis=1), jnp.concatenate(high, axis=1)], axis=0)
    inverse = lax.dot_general(both, at_slot, NT, preferred_element_type=F32)
    low_ref[...] = inverse[:PEERS].astype(I32)
    high_ref[...] = inverse[PEERS:].astype(I32)
    for copy in copies[1:]:
        copy.wait()
    meta_ref[8:16, :] = rank_ref[...]
    meta_ref[16:24, :] = target_ref[...]
    outer = lax.axis_index("sess") < BACKGROUND
    first = jnp.where(outer, BACKGROUND, 0)
    turns = jnp.where(outer, 1, 2)
    sub = iota((8, 128), 0)
    elems = elem_ref[...].astype(F32)

    def some_peers(turn, carry):
        for step in range(PEERS - BACKGROUND):
            peer = first + turn * (PEERS - BACKGROUND) + step
            index = jnp.broadcast_to(low_ref[pl.ds(peer, 1), :], (8, 128))
            part = jnp.broadcast_to(high_ref[pl.ds(peer, 1), :], (8, 128))
            for group in range(3):
                rows = slice(group * 8, group * 8 + 8)
                picked = lane_gather(weight_ref[rows, 0:128], index)
                for r in range(1, 8):
                    other = lane_gather(weight_ref[rows, r * 128 : r * 128 + 128], index)
                    picked = jnp.where(part == r, other, picked)
                send_ref[pl.ds(peer * 25 + group * 8, 8), :] = picked
            ids = jnp.where(sub == part, lane_gather(elems, index), 0.0)
            send_ref[pl.ds(peer * 25 + 24, 1), :] = jnp.sum(ids, axis=0, keepdims=True)
        return carry

    lax.fori_loop(0, turns, some_peers, 0)


def serve_kernel(recv_ref, split_ref, first_ref, reply_ref):
    outer = lax.axis_index("sess") < BACKGROUND
    first = jnp.where(outer, PEERS - 14, 0)
    turns = jnp.where(outer, 2, 3)
    elem_iota = iota((128, 128), 0)

    def seven_peers(turn, carry):
        peers = [first + turn * 7 + i for i in range(7)]
        hot, picks = [], []
        for peer in peers:
            index = recv_ref[pl.ds(peer * 25 + 24, 1), :].astype(I32)
            picks.append(jnp.broadcast_to(index, (8, 128)))
            hot.append(jnp.where(index == elem_iota, 1.0, 0.0).astype(BF16))
        hot = jnp.concatenate(hot, axis=1)
        hot = jnp.concatenate([hot, hot], axis=0)

        def weight(peer, i):
            return jnp.broadcast_to(recv_ref[pl.ds(peer * 25 + i, 1), :], (8, 128))

        for c in range(3):
            if c:
                rows = slice(c * 512 - 512, c * 512)
                picked = jnp.dot(split_ref[rows, :], hot, preferred_element_type=F32).reshape(8, 8, 8, 896)
            for i, peer in enumerate(peers):
                total = None
                for z in range(8):
                    line = None
                    for y in range(8):
                        if c:
                            term = picked[z, y, :, i * 128 : i * 128 + 128]
                        else:
                            term = lane_gather(first_ref[z, y], picks[i])
                        term = term * weight(peer, 8 + y)
                        line = term if line is None else line + term
                    line = line * weight(peer, z)
                    total = line if total is None else total + line
                wx = recv_ref[pl.ds(peer * 25 + 16, 8), :]
                reply_ref[pl.ds(peer * 3 + c, 1), :] = jnp.sum(total * wx, axis=0, keepdims=True)
        return carry

    lax.fori_loop(0, turns, seven_peers, 0)


def finish_kernel(reply_ref, meta_ref, value_ref, low_ref, high_ref):
    sub = iota((8, 128), 0)
    planes = [[reply_ref[pl.ds(g * 24 + c, 8, stride=3), :] for g in range(4)] for c in range(3)]
    values = [[], [], []]
    for r in range(8):
        index = jnp.broadcast_to(meta_ref[r : r + 1, :], (8, 128))
        rank = jnp.broadcast_to(meta_ref[8 + r : 9 + r, :], (8, 128))
        for c in range(3):
            total = jnp.zeros((8, 128), F32)
            for g in range(4):
                total = jnp.where(rank == sub + 8 * g, lane_gather(planes[c][g], index), total)
            values[c].append(jnp.sum(total, axis=0, keepdims=True))
    values = jnp.concatenate([jnp.concatenate(v, axis=1) for v in values], axis=0)
    value_ref[...] = values
    target = jnp.concatenate([meta_ref[16 + r : 17 + r, :] for r in range(8)], axis=1)
    elem = target >> 9
    zx = ((target >> 6) & 7) * 8 + (target & 7)
    y2 = ((target >> 3) & 7) * 2
    key = jnp.where(elem == 127, y2, jnp.where(elem == 0, y2 + 1, -1))
    left = jnp.where(zx == iota((64, 1024), 0), 1.0, 0.0).astype(BF16)
    hit = key == iota((16, 1024), 0)
    rows = jnp.concatenate([jnp.where(hit, values[c : c + 1], 0.0) for c in range(3)], axis=0)
    rows = jnp.concatenate([rows, jnp.zeros((16, 1024), F32)], axis=0)
    high, low = split2(rows)
    both = jnp.concatenate([high, low], axis=0)
    out = lax.dot_general(left, both, NT, preferred_element_type=F32)
    out = TAU * (out + pltpu.roll(out, 64, 1))
    low_ref[...] = out[:32]
    high_ref[...] = out[32:]


def ends_kernel(v_ref, c_ref, ends_ref, split_ref, first_ref):
    first_ref[...] = v_ref[0]
    lane = iota((8, 128), 1)
    for c in (1, 2):
        high, low = split2(v_ref[c].reshape(512, 128))
        split_ref[c * 512 - 512 : c * 512, 0:128] = high
        split_ref[c * 512 - 512 : c * 512, 128:256] = low
    for z in range(8):
        block = jnp.zeros((8, 128), F32)
        for c in range(3):
            for y in range(8):
                i = c * 8 + y
                rolled = pltpu.roll(v_ref[c, z, y], 2 * i + 1, 1)
                block = jnp.where((lane >> 1) == i, rolled, block)
        ends_ref[z * 8 : z * 8 + 8, :] = block
        block = jnp.zeros((8, 128), F32)
        for y in range(8):
            rolled = pltpu.roll(c_ref[z, y], 2 * y + 1, 1)
            block = jnp.where((lane >> 1) == y, rolled, block)
        block = block + pltpu.roll(block, 16, 1) + pltpu.roll(block, 32, 1)
        ends_ref[64 + z * 8 : 72 + z * 8, :] = block


def neighbour_sum(c_ref, kx, src, c, z, y, v):
    s = kx * pltpu.roll(v, 7, 0) + pltpu.roll(kx * v, 1, 0)
    if z < 7:
        s = s + c_ref[z, y] * src[c, z + 1, y]
    if z > 0:
        s = s + c_ref[z - 1, y] * src[c, z - 1, y]
    if y < 7:
        s = s + c_ref[z, y] * src[c, z, y + 1]
    if y > 0:
        s = s + c_ref[z, y - 1] * src[c, z, y - 1]
    return s


def local_diag(c_ref, z, y):
    kx = jnp.where(iota((8, 128), 0) < 7, c_ref[z, y], 0.0)
    d = H_MASS / H_STIFF + kx + pltpu.roll(kx, 1, 0)
    if z < 7:
        d = d + c_ref[z, y]
    if z > 0:
        d = d + c_ref[z - 1, y]
    if y < 7:
        d = d + c_ref[z, y]
    if y > 0:
        d = d + c_ref[z, y - 1]
    return d


def couple(lower, upper, lane):
    to_upper = upper + jnp.where(lane > 0, pltpu.roll(lower, 1, 1), 0.0)
    to_lower = lower + jnp.where(lane < 127, pltpu.roll(upper, 127, 1), 0.0)
    return to_lower, to_upper


def one_pass(c_ref, w_ref, dl_ref, rhs, src, dst, extra=None):
    lane = iota((8, 128), 1)
    sub = iota((8, 128), 0)

    def store(c, z, y, value):
        dst[c, z, y] = value if extra is None else value + extra[c, z, y]

    for y in range(8):
        for z in range(1, 7):
            kx = jnp.where(sub < 7, c_ref[z, y], 0.0)
            for c in range(3):
                v = src[c, z, y]
                s = rhs(c, z, y) + neighbour_sum(c_ref, kx, src, c, z, y, v)
                store(c, z, y, (1.0 - OMEGA) * v + w_ref[z, y] * s)
        k0 = jnp.where(sub < 7, c_ref[0, y], 0.0)
        k7 = jnp.where(sub < 7, c_ref[7, y], 0.0)
        for c in range(3):
            v0 = src[c, 0, y]
            v7 = src[c, 7, y]
            r0 = rhs(c, 0, y) + neighbour_sum(c_ref, k0, src, c, 0, y, v0) - dl_ref[0, y] * v0
            r7 = rhs(c, 7, y) + neighbour_sum(c_ref, k7, src, c, 7, y, v7) - dl_ref[1, y] * v7
            s7, s0 = couple(r7, r0, lane)
            store(c, 0, y, v0 + w_ref[0, y] * s0)
            store(c, 7, y, v7 + w_ref[7, y] * s7)


def edge_masks():
    blk = lax.axis_index("blk")
    even = (iota((8, 128), 1) & 1) == 0
    joined = (even & (blk < BLOCKS - 1)) | (jnp.logical_not(even) & (blk > 0))
    return even, joined


def edge_stack(own, below, above, offset, even):
    lower, upper = [], []
    for z in range(8):
        rows = slice(offset + z * 8, offset + z * 8 + 8)
        mine = own[rows, :]
        lower.append(jnp.where(even, mine, pltpu.roll(below[rows, :], 1, 1)))
        upper.append(jnp.where(even, pltpu.roll(above[rows, :], 127, 1), mine))
    return lower + upper


def edge_pass(number, v, rhs, k, ky, kx, w, d7, d8, joined):
    r = {}
    for i in range(1 + number, 15 - number):
        s = rhs[i]
        s = s + kx[i] * pltpu.roll(v[i], 7, 0) + pltpu.roll(kx[i] * v[i], 1, 0)
        s = s + ky[i] * pltpu.roll(v[i], 126, 1) + pltpu.roll(ky[i] * v[i], 2, 1)
        if i % 8 < 7:
            s = s + k[i] * v[i + 1]
        if i % 8 > 0:
            s = s + k[i - 1] * v[i - 1]
        if i == 7:
            s = s - d7 * v[i]
        if i == 8:
            s = s - d8 * v[i]
        r[i] = s
    r[7], r[8] = r[7] + jnp.where(joined, r[8], 0.0), r[8] + jnp.where(joined, r[7], 0.0)
    return {i: (v[i] if i in (7, 8) else (1.0 - OMEGA) * v[i]) + w[i] * r[i] for i in r}


def base_kernel(v_ref, c_ref, meta_ref, out_ref, w_ref, node_ref, buf_ref, dl_ref):
    lane = iota((8, 128), 1)
    target = jnp.concatenate([meta_ref[16 + r : 17 + r, :] for r in range(8)], axis=1)
    node_ref[...] = jnp.where((target & 511) == iota((512, 1024), 0), 1.0, 0.0).astype(BF16)
    for y in range(8):
        diags = [local_diag(c_ref, z, y) for z in range(8)]
        dl_ref[0, y] = diags[0]
        dl_ref[1, y] = diags[7]
        diags[7], diags[0] = couple(diags[7], diags[0], lane)
        for z in range(8):
            w_ref[z, y] = OMEGA / diags[z]

    def rhs(c, z, y):
        return (H_MASS / H_STIFF) * v_ref[c, z, y]

    coefs = (c_ref, w_ref, dl_ref, rhs)
    one_pass(*coefs, v_ref, buf_ref)
    one_pass(*coefs, buf_ref, out_ref)
    one_pass(*coefs, out_ref, buf_ref)
    one_pass(*coefs, buf_ref, out_ref)


def prepare_edge(own_ref, below_ref, above_ref, edge_ref):
    even, joined = edge_masks()
    sub = iota((8, 128), 0)
    y_of = (iota((8, 128), 1) >> 1) & 7
    v = edge_stack(own_ref, below_ref, above_ref, 0, even)
    k = [H_STIFF * c for c in edge_stack(own_ref, below_ref, above_ref, 64, even)]
    ky = [jnp.where(y_of < 7, k[i], 0.0) for i in range(16)]
    kx = [jnp.where(sub < 7, k[i], 0.0) for i in range(16)]
    diag = []
    for i in range(16):
        d = H_MASS + kx[i] + pltpu.roll(kx[i], 1, 0) + ky[i] + pltpu.roll(ky[i], 2, 1)
        if i % 8 < 7:
            d = d + k[i]
        if i % 8 > 0:
            d = d + k[i - 1]
        diag.append(d)
    d7, d8 = diag[7], diag[8]
    edge_ref[5, 0] = d7
    edge_ref[5, 1] = d8
    diag[7], diag[8] = d7 + jnp.where(joined, d8, 0.0), d8 + jnp.where(joined, d7, 0.0)
    for i in range(16):
        edge_ref[0, i] = v[i]
        edge_ref[1, i] = k[i]
        edge_ref[2, i] = ky[i]
        edge_ref[3, i] = kx[i]
        edge_ref[4, i] = OMEGA / diag[i]


def main_kernel(
    value_ref,
    meta_ref,
    node_ref,
    base_ref,
    w_ref,
    c_ref,
    own_ref,
    below_ref,
    above_ref,
    value_out_ref,
    out_ref,
    edge_ref,
    add_ref,
    one_ref,
    two_ref,
    dl_ref,
):
    lane = iota((8, 128), 1)
    value_out_ref[...] = value_ref[...]
    prepare_edge(own_ref, below_ref, above_ref, edge_ref)
    target = jnp.concatenate([meta_ref[16 + r : 17 + r, :] for r in range(8)], axis=1)
    elem_hot = jnp.where((target >> 9) == iota((128, 1024), 0), 1.0, 0.0).astype(BF16)
    for c in range(3):
        value = (TAU / H_STIFF) * value_ref[c : c + 1, :]
        high, low = split2(jnp.broadcast_to(value, (16, 1024)))
        high = elem_hot * jnp.concatenate([high] * 8, axis=0)
        low = elem_hot * jnp.concatenate([low] * 8, axis=0)
        both = jnp.concatenate([high, low], axis=0)
        out = lax.dot_general(node_ref[...], both, NT, preferred_element_type=F32)
        add_ref[c] = (out[:, :128] + out[:, 128:]).reshape(8, 8, 8, 128)
    for y in range(8):
        dl_ref[0, y] = local_diag(c_ref, 0, y)
        dl_ref[1, y] = local_diag(c_ref, 7, y)
        for z in range(1, 7):
            for c in range(3):
                one_ref[c, z, y] = w_ref[z, y] * add_ref[c, z, y]
        for c in range(3):
            s7, s0 = couple(add_ref[c, 7, y], add_ref[c, 0, y], lane)
            one_ref[c, 0, y] = w_ref[0, y] * s0
            one_ref[c, 7, y] = w_ref[7, y] * s7

    def rhs(c, z, y):
        return add_ref[c, z, y]

    coefs = (c_ref, w_ref, dl_ref, rhs)
    one_pass(*coefs, one_ref, two_ref)
    one_pass(*coefs, two_ref, one_ref)
    one_pass(*coefs, one_ref, out_ref, base_ref)


def edge_kernel(
    main_ref, edge_ref, low_ref, high_ref, add_below_ref, add_above_ref, out_hbm, out_ref, sems
):
    lane = iota((8, 128), 1)
    even, joined = edge_masks()
    v, k, ky, kx, w = [[edge_ref[n, i] for i in range(16)] for n in range(5)]
    d7, d8 = edge_ref[5, 0], edge_ref[5, 1]
    rhs = [H_MASS * v[i] for i in range(16)]
    for z in range(8):
        part, rows = (low_ref, high_ref)[z // 4], slice(z % 4 * 8, z % 4 * 8 + 8)
        mine = part[rows, :]
        lower, upper = jnp.where(even, mine, 0.0), jnp.where(even, 0.0, mine)
        if z >= 4:
            lower = jnp.where(even, mine, pltpu.roll(add_below_ref[rows, :], 1, 1))
        else:
            upper = jnp.where(even, pltpu.roll(add_above_ref[rows, :], 127, 1), mine)
        rhs[z] = rhs[z] + lower
        rhs[8 + z] = rhs[8 + z] + upper
    now = v
    for number in range(NPASS):
        now = edge_pass(number, now, rhs, k, ky, kx, w, d7, d8, joined)
    copies = []
    for c in range(3):
        for half in range(2):
            planes = slice(half * 4, half * 4 + 4)
            for y in range(8):
                back = (127 - 2 * (c * 8 + y)) % 128
                where = lane == (0, 127)[half]
                for z in range(half * 4, half * 4 + 4):
                    new = pltpu.roll(now[z] if half else now[8 + z], back, 1)
                    out_ref[c, z, y] = jnp.where(where, new, main_ref[c, z, y])
            copies.append(
                pltpu.make_async_copy(
                    out_ref.at[c, planes], out_hbm.at[c, planes], sems.at[2 * c + half]
                )
            )
            copies[-1].start()
    for copy in copies:
        copy.wait()


def exchange(rows, count):
    chunks = rows.reshape(PEERS, count, 1, 128)
    return lax.all_to_all(chunks, "sess", 0, 0, tiled=True).reshape(PEERS * count, 128)


def call(kernel, outs, args, scratch=(), limit=24, space=pltpu.VMEM, out_space=pltpu.VMEM):
    single = len(outs) == 1
    spec = pl.BlockSpec(memory_space=out_space)
    return pl.pallas_call(
        kernel,
        out_shape=outs[0] if single else outs,
        in_specs=[pl.BlockSpec(memory_space=space)] * len(args),
        out_specs=spec if single else [spec] * len(outs),
        scratch_shapes=list(scratch),
        compiler_params=pltpu.CompilerParams(vmem_limit_bytes=limit * 1024 * 1024),
    )(*args)


def sds(*shape, dtype=F32):
    return jax.ShapeDtypeStruct(shape, dtype)


def body(velocity_old, conductance, donor_rank, donor_elem, target_node, iface_weights):
    rank = donor_rank.reshape(8, 128)
    elem = donor_elem.reshape(8, 128)
    target = target_node.reshape(8, 128)
    weights = iface_weights.reshape(24, 1024)
    send, meta = call(
        pack_kernel,
        [sds(PEERS * 25, 128), sds(24, 128, dtype=I32)],
        [rank, elem, weights, target],
        [
            pltpu.VMEM((8, 128), I32),
            pltpu.VMEM((8, 128), I32),
            pltpu.VMEM((24, 1024), F32),
            pltpu.VMEM((8, 128), I32),
            pltpu.VMEM((PEERS, 128), I32),
            pltpu.VMEM((PEERS, 128), I32),
            pltpu.SemaphoreType.DMA((4,)),
        ],
        space=pl.ANY,
        limit=56,
    )
    up = [(i, (i + 1) % BLOCKS) for i in range(BLOCKS)]
    down = [(j, i) for i, j in up]
    recv = exchange(send, 25)
    plane = (8, 8, 8, 128)
    own, split, first = call(
        ends_kernel,
        [sds(128, 128), sds(1024, 256, dtype=BF16), sds(*plane)],
        [velocity_old, conductance],
    )
    below = lax.ppermute(own, "blk", up)
    above = lax.ppermute(own, "blk", down)
    recv, below, above = lax.optimization_barrier((recv, below, above))
    reply = call(serve_kernel, [sds(PEERS * 3, 128)], [recv, split, first])
    reply, v_later, c_later = lax.optimization_barrier((reply, velocity_old, conductance))
    reply = exchange(reply, 3)
    base, w, nodes = call(
        base_kernel,
        [sds(3, *plane), sds(*plane), sds(512, 1024, dtype=BF16)],
        [v_later, c_later, meta],
        [pltpu.VMEM((3,) + plane, F32), pltpu.VMEM((2, 8, 8, 128), F32)],
    )
    reply, base, w, nodes = lax.optimization_barrier((reply, base, w, nodes))
    values, add_low, add_high = call(
        finish_kernel, [sds(3, 1024), sds(32, 128), sds(32, 128)], [reply, meta]
    )
    add_below = lax.ppermute(add_high, "blk", up)
    add_above = lax.ppermute(add_low, "blk", down)
    iface_values, main, edge = call(
        main_kernel,
        [sds(3, 1024), sds(3, *plane), sds(6, 16, 8, 128)],
        [values, meta, nodes, base, w, c_later, own, below, above],
        [pltpu.VMEM((3,) + plane, F32)] * 3 + [pltpu.VMEM((2, 8, 8, 128), F32)],
    )
    field = call(
        edge_kernel,
        [sds(3, *plane)],
        [main, edge, add_low, add_high, add_below, add_above],
        [pltpu.VMEM((3,) + plane, F32), pltpu.SemaphoreType.DMA((6,))],
        out_space=pl.ANY,
    )
    return field, iface_values


def solution(mesh):
    in_specs = (
        P(None, None, None, None, ("sess", "blk")),
        P(None, None, None, ("sess", "blk")),
        P(("sess", "blk")),
        P(("sess", "blk")),
        P(("sess", "blk")),
        P(None, None, ("sess", "blk")),
    )
    out_specs = (P(None, None, None, None, ("sess", "blk")), P(None, ("sess", "blk")))
    return jax.shard_map(body, mesh=mesh, in_specs=in_specs, out_specs=out_specs, check_vma=False)
```

```python
import jax
import jax.numpy as jnp
from jax import lax
from jax.experimental import pallas as pl
from jax.experimental.pallas import tpu as pltpu
from jax.sharding import PartitionSpec as P

NPASS = 4
H_MASS = 1.0
H_STIFF = 4.0
OMEGA = 0.6
TAU = 8.0
PEERS = 32
BLOCKS = 8
BACKGROUND = 21
F32 = jnp.float32
BF16 = jnp.bfloat16
I32 = jnp.int32
NT = (((1,), (1,)), ((), ()))


def iota(shape, dim):
    return lax.broadcasted_iota(I32, shape, dim)


def lane_gather(values, index):
    return jnp.take_along_axis(values, index, axis=1)


def split2(values):
    high = values.astype(BF16)
    return high, (values - high.astype(F32)).astype(BF16)


def pack_kernel(
    rank_hbm, elem_hbm, weight_hbm, target_hbm, send_ref, meta_ref, rank_ref, elem_ref, weight_ref, target_ref, low_ref, high_ref, sems
):
    copies = [
        pltpu.make_async_copy(rank_hbm, rank_ref, sems.at[0]),
        pltpu.make_async_copy(elem_hbm, elem_ref, sems.at[1]),
        pltpu.make_async_copy(weight_hbm, weight_ref, sems.at[2]),
        pltpu.make_async_copy(target_hbm, target_ref, sems.at[3]),
    ]
    for copy in copies:
        copy.start()
    copies[0].wait()
    rank_iota = iota((PEERS, 128), 0)
    row = iota((128, 256), 0)
    col = iota((128, 256), 1)
    upper = jnp.where((row < col) | (col >= 128), 1.0, 0.0).astype(BF16)
    hits = [rank_ref[r : r + 1, :] == rank_iota for r in range(8)]
    hot = jnp.concatenate([jnp.where(hit, 1.0, 0.0).astype(BF16) for hit in hits], axis=0)
    counts = jnp.dot(hot, upper, preferred_element_type=F32)
    offset = jnp.zeros((PEERS, 128), F32)
    pos_iota = iota((128, 128), 0)
    lane = iota((PEERS, 128), 1).astype(F32)
    at_slot, low, high = [], [], []
    for r in range(8):
        mine = counts[r * PEERS : (r + 1) * PEERS]
        place = jnp.where(hits[r], mine[:, :128] + offset, 0.0)
        pos = jnp.sum(place, axis=0, keepdims=True).astype(I32)
        offset = offset + mine[:, 128:]
        meta_ref[r : r + 1, :] = pos
        at_slot.append(jnp.where(pos == pos_iota, 1.0, 0.0).astype(BF16))
        low.append(jnp.where(hits[r], lane, 0.0).astype(BF16))
        high.append(jnp.where(hits[r], float(r), 0.0).astype(BF16))
    at_slot = jnp.concatenate(at_slot, axis=1)
    both = jnp.concatenate([jnp.concatenate(low, axis=1), jnp.concatenate(high, axis=1)], axis=0)
    inverse = lax.dot_general(both, at_slot, NT, preferred_element_type=F32)
    low_ref[...] = inverse[:PEERS].astype(I32)
    high_ref[...] = inverse[PEERS:].astype(I32)
    for copy in copies[1:]:
        copy.wait()
    meta_ref[8:16, :] = rank_ref[...]
    meta_ref[16:24, :] = target_ref[...]
    outer = lax.axis_index("sess") < BACKGROUND
    first = jnp.where(outer, BACKGROUND, 0)
    turns = jnp.where(outer, 1, 2)
    sub = iota((8, 128), 0)
    elems = elem_ref[...].astype(F32)

    def some_peers(turn, carry):
        for step in range(PEERS - BACKGROUND):
            peer = first + turn * (PEERS - BACKGROUND) + step
            index = jnp.broadcast_to(low_ref[pl.ds(peer, 1), :], (8, 128))
            part = jnp.broadcast_to(high_ref[pl.ds(peer, 1), :], (8, 128))
            for group in range(3):
                rows = slice(group * 8, group * 8 + 8)
                picked = lane_gather(weight_ref[rows, 0:128], index)
                for r in range(1, 8):
                    other = lane_gather(weight_ref[rows, r * 128 : r * 128 + 128], index)
                    picked = jnp.where(part == r, other, picked)
                send_ref[pl.ds(peer * 25 + group * 8, 8), :] = picked
            ids = jnp.where(sub == part, lane_gather(elems, index), 0.0)
            send_ref[pl.ds(peer * 25 + 24, 1), :] = jnp.sum(ids, axis=0, keepdims=True)
        return carry

    lax.fori_loop(0, turns, some_peers, 0)


def serve_kernel(recv_ref, split_ref, first_ref, reply_ref):
    outer = lax.axis_index("sess") < BACKGROUND
    first = jnp.where(outer, PEERS - 14, 0)
    turns = jnp.where(outer, 2, 3)
    elem_iota = iota((128, 128), 0)

    def seven_peers(turn, carry):
        peers = [first + turn * 7 + i for i in range(7)]
        hot, picks = [], []
        for peer in peers:
            index = recv_ref[pl.ds(peer * 25 + 24, 1), :].astype(I32)
            picks.append(jnp.broadcast_to(index, (8, 128)))
            hot.append(jnp.where(index == elem_iota, 1.0, 0.0).astype(BF16))
        hot = jnp.concatenate(hot, axis=1)
        hot = jnp.concatenate([hot, hot], axis=0)

        def weight(peer, i):
            return jnp.broadcast_to(recv_ref[pl.ds(peer * 25 + i, 1), :], (8, 128))

        for c in range(3):
            if c:
                rows = slice(c * 512 - 512, c * 512)
                picked = jnp.dot(split_ref[rows, :], hot, preferred_element_type=F32).reshape(8, 8, 8, 896)
            for i, peer in enumerate(peers):
                total = None
                for z in range(8):
                    line = None
                    for y in range(8):
                        if c:
                            term = picked[z, y, :, i * 128 : i * 128 + 128]
                        else:
                            term = lane_gather(first_ref[z, y], picks[i])
                        term = term * weight(peer, 8 + y)
                        line = term if line is None else line + term
                    line = line * weight(peer, z)
                    total = line if total is None else total + line
                wx = recv_ref[pl.ds(peer * 25 + 16, 8), :]
                reply_ref[pl.ds(peer * 3 + c, 1), :] = jnp.sum(total * wx, axis=0, keepdims=True)
        return carry

    lax.fori_loop(0, turns, seven_peers, 0)


def finish_kernel(reply_ref, meta_ref, value_ref, low_ref, high_ref):
    sub = iota((8, 128), 0)
    planes = [[reply_ref[pl.ds(g * 24 + c, 8, stride=3), :] for g in range(4)] for c in range(3)]
    values = [[], [], []]
    for r in range(8):
        index = jnp.broadcast_to(meta_ref[r : r + 1, :], (8, 128))
        rank = jnp.broadcast_to(meta_ref[8 + r : 9 + r, :], (8, 128))
        for c in range(3):
            total = jnp.zeros((8, 128), F32)
            for g in range(4):
                total = jnp.where(rank == sub + 8 * g, lane_gather(planes[c][g], index), total)
            values[c].append(jnp.sum(total, axis=0, keepdims=True))
    values = jnp.concatenate([jnp.concatenate(v, axis=1) for v in values], axis=0)
    value_ref[...] = values
    target = jnp.concatenate([meta_ref[16 + r : 17 + r, :] for r in range(8)], axis=1)
    elem = target >> 9
    zx = ((target >> 6) & 7) * 8 + (target & 7)
    y2 = ((target >> 3) & 7) * 2
    key = jnp.where(elem == 127, y2, jnp.where(elem == 0, y2 + 1, -1))
    left = jnp.where(zx == iota((64, 1024), 0), 1.0, 0.0).astype(BF16)
    hit = key == iota((16, 1024), 0)
    rows = jnp.concatenate([jnp.where(hit, values[c : c + 1], 0.0) for c in range(3)], axis=0)
    rows = jnp.concatenate([rows, jnp.zeros((16, 1024), F32)], axis=0)
    high, low = split2(rows)
    both = jnp.concatenate([high, low], axis=0)
    out = lax.dot_general(left, both, NT, preferred_element_type=F32)
    out = TAU * (out + pltpu.roll(out, 64, 1))
    low_ref[...] = out[:32]
    high_ref[...] = out[32:]


def ends_kernel(v_ref, c_ref, ends_ref, split_ref, first_ref):
    first_ref[...] = v_ref[0]
    lane = iota((8, 128), 1)
    for c in (1, 2):
        high, low = split2(v_ref[c].reshape(512, 128))
        split_ref[c * 512 - 512 : c * 512, 0:128] = high
        split_ref[c * 512 - 512 : c * 512, 128:256] = low
    for z in range(8):
        block = jnp.zeros((8, 128), F32)
        for c in range(3):
            for y in range(8):
                i = c * 8 + y
                rolled = pltpu.roll(v_ref[c, z, y], 2 * i + 1, 1)
                block = jnp.where((lane >> 1) == i, rolled, block)
        ends_ref[z * 8 : z * 8 + 8, :] = block
        block = jnp.zeros((8, 128), F32)
        for y in range(8):
            rolled = pltpu.roll(c_ref[z, y], 2 * y + 1, 1)
            block = jnp.where((lane >> 1) == y, rolled, block)
        block = block + pltpu.roll(block, 16, 1) + pltpu.roll(block, 32, 1)
        ends_ref[64 + z * 8 : 72 + z * 8, :] = block


def neighbour_sum(c_ref, kx, src, c, z, y, v):
    s = kx * pltpu.roll(v, 7, 0) + pltpu.roll(kx * v, 1, 0)
    if z < 7:
        s = s + c_ref[z, y] * src[c, z + 1, y]
    if z > 0:
        s = s + c_ref[z - 1, y] * src[c, z - 1, y]
    if y < 7:
        s = s + c_ref[z, y] * src[c, z, y + 1]
    if y > 0:
        s = s + c_ref[z, y - 1] * src[c, z, y - 1]
    return s


def local_diag(c_ref, z, y):
    kx = jnp.where(iota((8, 128), 0) < 7, c_ref[z, y], 0.0)
    d = H_MASS / H_STIFF + kx + pltpu.roll(kx, 1, 0)
    if z < 7:
        d = d + c_ref[z, y]
    if z > 0:
        d = d + c_ref[z - 1, y]
    if y < 7:
        d = d + c_ref[z, y]
    if y > 0:
        d = d + c_ref[z, y - 1]
    return d


def couple(lower, upper, lane):
    to_upper = upper + jnp.where(lane > 0, pltpu.roll(lower, 1, 1), 0.0)
    to_lower = lower + jnp.where(lane < 127, pltpu.roll(upper, 127, 1), 0.0)
    return to_lower, to_upper


def one_pass(c_ref, w_ref, dl_ref, rhs, src, dst, extra=None):
    lane = iota((8, 128), 1)
    sub = iota((8, 128), 0)

    def store(c, z, y, value):
        dst[c, z, y] = value if extra is None else value + extra[c, z, y]

    for y in range(8):
        for z in range(1, 7):
            kx = jnp.where(sub < 7, c_ref[z, y], 0.0)
            for c in range(3):
                v = src[c, z, y]
                s = rhs(c, z, y) + neighbour_sum(c_ref, kx, src, c, z, y, v)
                store(c, z, y, (1.0 - OMEGA) * v + w_ref[z, y] * s)
        k0 = jnp.where(sub < 7, c_ref[0, y], 0.0)
        k7 = jnp.where(sub < 7, c_ref[7, y], 0.0)
        for c in range(3):
            v0 = src[c, 0, y]
            v7 = src[c, 7, y]
            r0 = rhs(c, 0, y) + neighbour_sum(c_ref, k0, src, c, 0, y, v0) - dl_ref[0, y] * v0
            r7 = rhs(c, 7, y) + neighbour_sum(c_ref, k7, src, c, 7, y, v7) - dl_ref[1, y] * v7
            s7, s0 = couple(r7, r0, lane)
            store(c, 0, y, v0 + w_ref[0, y] * s0)
            store(c, 7, y, v7 + w_ref[7, y] * s7)


def edge_masks():
    blk = lax.axis_index("blk")
    even = (iota((8, 128), 1) & 1) == 0
    joined = (even & (blk < BLOCKS - 1)) | (jnp.logical_not(even) & (blk > 0))
    return even, joined


def edge_stack(own, below, above, offset, even):
    lower, upper = [], []
    for z in range(8):
        rows = slice(offset + z * 8, offset + z * 8 + 8)
        mine = own[rows, :]
        lower.append(jnp.where(even, mine, pltpu.roll(below[rows, :], 1, 1)))
        upper.append(jnp.where(even, pltpu.roll(above[rows, :], 127, 1), mine))
    return lower + upper


def edge_pass(number, v, rhs, k, ky, kx, w, d7, d8, joined):
    r = {}
    for i in range(1 + number, 15 - number):
        s = rhs[i]
        s = s + kx[i] * pltpu.roll(v[i], 7, 0) + pltpu.roll(kx[i] * v[i], 1, 0)
        s = s + ky[i] * pltpu.roll(v[i], 126, 1) + pltpu.roll(ky[i] * v[i], 2, 1)
        if i % 8 < 7:
            s = s + k[i] * v[i + 1]
        if i % 8 > 0:
            s = s + k[i - 1] * v[i - 1]
        if i == 7:
            s = s - d7 * v[i]
        if i == 8:
            s = s - d8 * v[i]
        r[i] = s
    r[7], r[8] = r[7] + jnp.where(joined, r[8], 0.0), r[8] + jnp.where(joined, r[7], 0.0)
    return {i: (v[i] if i in (7, 8) else (1.0 - OMEGA) * v[i]) + w[i] * r[i] for i in r}


def base_kernel(v_ref, c_ref, meta_ref, out_ref, w_ref, node_ref, buf_ref, dl_ref):
    lane = iota((8, 128), 1)
    target = jnp.concatenate([meta_ref[16 + r : 17 + r, :] for r in range(8)], axis=1)
    node_ref[...] = jnp.where((target & 511) == iota((512, 1024), 0), 1.0, 0.0).astype(BF16)
    for y in range(8):
        diags = [local_diag(c_ref, z, y) for z in range(8)]
        dl_ref[0, y] = diags[0]
        dl_ref[1, y] = diags[7]
        diags[7], diags[0] = couple(diags[7], diags[0], lane)
        for z in range(8):
            w_ref[z, y] = OMEGA / diags[z]

    def rhs(c, z, y):
        return (H_MASS / H_STIFF) * v_ref[c, z, y]

    coefs = (c_ref, w_ref, dl_ref, rhs)
    one_pass(*coefs, v_ref, buf_ref)
    one_pass(*coefs, buf_ref, out_ref)
    one_pass(*coefs, out_ref, buf_ref)
    one_pass(*coefs, buf_ref, out_ref)


def main_kernel(value_ref, meta_ref, node_ref, base_ref, w_ref, c_ref, out_ref, add_ref, one_ref, two_ref, dl_ref):
    lane = iota((8, 128), 1)
    target = jnp.concatenate([meta_ref[16 + r : 17 + r, :] for r in range(8)], axis=1)
    elem_hot = jnp.where((target >> 9) == iota((128, 1024), 0), 1.0, 0.0).astype(BF16)
    for c in range(3):
        value = (TAU / H_STIFF) * value_ref[c : c + 1, :]
        high, low = split2(jnp.broadcast_to(value, (16, 1024)))
        high = elem_hot * jnp.concatenate([high] * 8, axis=0)
        low = elem_hot * jnp.concatenate([low] * 8, axis=0)
        both = jnp.concatenate([high, low], axis=0)
        out = lax.dot_general(node_ref[...], both, NT, preferred_element_type=F32)
        add_ref[c] = (out[:, :128] + out[:, 128:]).reshape(8, 8, 8, 128)
    for y in range(8):
        dl_ref[0, y] = local_diag(c_ref, 0, y)
        dl_ref[1, y] = local_diag(c_ref, 7, y)
        for z in range(1, 7):
            for c in range(3):
                one_ref[c, z, y] = w_ref[z, y] * add_ref[c, z, y]
        for c in range(3):
            s7, s0 = couple(add_ref[c, 7, y], add_ref[c, 0, y], lane)
            one_ref[c, 0, y] = w_ref[0, y] * s0
            one_ref[c, 7, y] = w_ref[7, y] * s7

    def rhs(c, z, y):
        return add_ref[c, z, y]

    coefs = (c_ref, w_ref, dl_ref, rhs)
    one_pass(*coefs, one_ref, two_ref)
    one_pass(*coefs, two_ref, one_ref)
    one_pass(*coefs, one_ref, out_ref, base_ref)


def edge_kernel(
    main_ref,
    own_ref,
    below_ref,
    above_ref,
    low_ref,
    high_ref,
    add_below_ref,
    add_above_ref,
    value_ref,
    out_hbm,
    value_hbm,
    out_ref,
    sems,
):
    copies = [pltpu.make_async_copy(value_ref, value_hbm, sems.at[6])]
    copies[0].start()
    lane = iota((8, 128), 1)
    sub = iota((8, 128), 0)
    even, joined = edge_masks()
    y_of = (lane >> 1) & 7
    v = edge_stack(own_ref, below_ref, above_ref, 0, even)
    k = [H_STIFF * c for c in edge_stack(own_ref, below_ref, above_ref, 64, even)]
    rhs = [H_MASS * v[i] for i in range(16)]
    for z in range(8):
        part, rows = (low_ref, high_ref)[z // 4], slice(z % 4 * 8, z % 4 * 8 + 8)
        mine = part[rows, :]
        lower, upper = jnp.where(even, mine, 0.0), jnp.where(even, 0.0, mine)
        if z >= 4:
            lower = jnp.where(even, mine, pltpu.roll(add_below_ref[rows, :], 1, 1))
        else:
            upper = jnp.where(even, pltpu.roll(add_above_ref[rows, :], 127, 1), mine)
        rhs[z] = rhs[z] + lower
        rhs[8 + z] = rhs[8 + z] + upper
    ky = [jnp.where(y_of < 7, k[i], 0.0) for i in range(16)]
    kx = [jnp.where(sub < 7, k[i], 0.0) for i in range(16)]
    diag = []
    for i in range(16):
        d = H_MASS + kx[i] + pltpu.roll(kx[i], 1, 0) + ky[i] + pltpu.roll(ky[i], 2, 1)
        if i % 8 < 7:
            d = d + k[i]
        if i % 8 > 0:
            d = d + k[i - 1]
        diag.append(d)
    d7, d8 = diag[7], diag[8]
    diag[7], diag[8] = d7 + jnp.where(joined, d8, 0.0), d8 + jnp.where(joined, d7, 0.0)
    w = [OMEGA / d for d in diag]
    now = v
    for number in range(NPASS):
        now = edge_pass(number, now, rhs, k, ky, kx, w, d7, d8, joined)
    for c in range(3):
        for half in range(2):
            planes = slice(half * 4, half * 4 + 4)
            for y in range(8):
                back = (127 - 2 * (c * 8 + y)) % 128
                where = lane == (0, 127)[half]
                for z in range(half * 4, half * 4 + 4):
                    new = pltpu.roll(now[z] if half else now[8 + z], back, 1)
                    out_ref[c, z, y] = jnp.where(where, new, main_ref[c, z, y])
            copies.append(
                pltpu.make_async_copy(
                    out_ref.at[c, planes], out_hbm.at[c, planes], sems.at[2 * c + half]
                )
            )
            copies[-1].start()
    for copy in copies:
        copy.wait()


def exchange(rows, count):
    chunks = rows.reshape(PEERS, count, 1, 128)
    return lax.all_to_all(chunks, "sess", 0, 0, tiled=True).reshape(PEERS * count, 128)


def call(kernel, outs, args, scratch=(), limit=24, space=pltpu.VMEM, out_space=pltpu.VMEM):
    single = len(outs) == 1
    spec = pl.BlockSpec(memory_space=out_space)
    return pl.pallas_call(
        kernel,
        out_shape=outs[0] if single else outs,
        in_specs=[pl.BlockSpec(memory_space=space)] * len(args),
        out_specs=spec if single else [spec] * len(outs),
        scratch_shapes=list(scratch),
        compiler_params=pltpu.CompilerParams(vmem_limit_bytes=limit * 1024 * 1024),
    )(*args)


def sds(*shape, dtype=F32):
    return jax.ShapeDtypeStruct(shape, dtype)


def body(velocity_old, conductance, donor_rank, donor_elem, target_node, iface_weights):
    rank = donor_rank.reshape(8, 128)
    elem = donor_elem.reshape(8, 128)
    target = target_node.reshape(8, 128)
    weights = iface_weights.reshape(24, 1024)
    send, meta = call(
        pack_kernel,
        [sds(PEERS * 25, 128), sds(24, 128, dtype=I32)],
        [rank, elem, weights, target],
        [
            pltpu.VMEM((8, 128), I32),
            pltpu.VMEM((8, 128), I32),
            pltpu.VMEM((24, 1024), F32),
            pltpu.VMEM((8, 128), I32),
            pltpu.VMEM((PEERS, 128), I32),
            pltpu.VMEM((PEERS, 128), I32),
            pltpu.SemaphoreType.DMA((4,)),
        ],
        space=pl.ANY,
        limit=56,
    )
    up = [(i, (i + 1) % BLOCKS) for i in range(BLOCKS)]
    down = [(j, i) for i, j in up]
    recv = exchange(send, 25)
    plane = (8, 8, 8, 128)
    own, split, first = call(
        ends_kernel,
        [sds(128, 128), sds(1024, 256, dtype=BF16), sds(*plane)],
        [velocity_old, conductance],
    )
    below = lax.ppermute(own, "blk", up)
    above = lax.ppermute(own, "blk", down)
    recv, below, above = lax.optimization_barrier((recv, below, above))
    reply = call(serve_kernel, [sds(PEERS * 3, 128)], [recv, split, first])
    reply, v_later, c_later = lax.optimization_barrier((reply, velocity_old, conductance))
    reply = exchange(reply, 3)
    base, w, nodes = call(
        base_kernel,
        [sds(3, *plane), sds(*plane), sds(512, 1024, dtype=BF16)],
        [v_later, c_later, meta],
        [pltpu.VMEM((3,) + plane, F32), pltpu.VMEM((2, 8, 8, 128), F32)],
    )
    reply, base, w, nodes = lax.optimization_barrier((reply, base, w, nodes))
    values, add_low, add_high = call(
        finish_kernel, [sds(3, 1024), sds(32, 128), sds(32, 128)], [reply, meta]
    )
    add_below = lax.ppermute(add_high, "blk", up)
    add_above = lax.ppermute(add_low, "blk", down)
    main = call(
        main_kernel,
        [sds(3, *plane)],
        [values, meta, nodes, base, w, c_later],
        [pltpu.VMEM((3,) + plane, F32)] * 3 + [pltpu.VMEM((2, 8, 8, 128), F32)],
    )
    field, iface_values = call(
        edge_kernel,
        [sds(3, *plane), sds(3, 1024)],
        [main, own, below, above, add_low, add_high, add_below, add_above, values],
        [pltpu.VMEM((3,) + plane, F32), pltpu.SemaphoreType.DMA((7,))],
        out_space=pl.ANY,
    )
    return field, iface_values


def solution(mesh):
    in_specs = (
        P(None, None, None, None, ("sess", "blk")),
        P(None, None, None, ("sess", "blk")),
        P(("sess", "blk")),
        P(("sess", "blk")),
        P(("sess", "blk")),
        P(None, None, ("sess", "blk")),
    )
    out_specs = (P(None, None, None, None, ("sess", "blk")), P(None, ("sess", "blk")))
    return jax.shard_map(body, mesh=mesh, in_specs=in_specs, out_specs=out_specs, check_vma=False)
```
